256 devices in a mesh: date: 128 (over x_lo, z, y, core), row: 2 (over x_hi).
Axes of the slice: x: 4 (x_hi: 2, x_lo: 2; x = x_hi * 2 + x_lo), y: 4, z: 8, core: 2. Of those that a mesh axis runs over, the one named last changes fastest.
Arguments:
- slc: bfloat16 [128, 2, 160, 2560], P('date', None, 'row'), may hold values from -6 to 6
- coarse: int32 [128, 2], P('date'), may hold values from -8 to 8, as said below
- fraction: int32 [128, 2], P('date'), may hold values from 0 to 63
- pair_on: int32 [128, 3], P('date'), may hold values 0 or 1
- ref_date: int32 [1], replicated, may hold values from 0 to 127
Outputs:
- ref_ifg: float32 [128, 2, 32, 128], P('date', None, 'row')
- pair_ifg: float32 [128, 3, 2, 32, 128], P('date', None, None, 'row')
- coherence: float32 [128, 3, 32, 128], P('date', None, 'row')
The draws below stay inside these ranges and needn't reach their ends.
Inputs may be any that keep to these rules, and one draw needn't show every extreme that they name: `coarse`: some date has row offset 8 and some other date row offset -8.
All inputs are finite; a program needn't handle non-finite values. No bound on the sum of `pair_on` on one device may be relied on, other than what follows from the above.
Results may differ from the reference program's by a relative error of at most 0.0075.
Values may be sent and summed in bfloat16 or wider, within the bound.
No kernel may reach another device: no remote copies, remote signals or barrier semaphores. Data moves between devices by JAX's collectives and lax.ppermute only.
A program may use at most 64 MiB of HBM per device.

```python
import jax
import jax.numpy as jnp
from jax import lax

COLS = 2560
MAXOFF = 8
NFRAC = 64
SPAN = 3
LOOK_R = 5
LOOK_C = 20
DATES = 128
WROWS = 160
HALO = 12


def draw_coarse(key, part):
    key = jax.random.fold_in(key, 11)
    values = jax.random.randint(key, (DATES, 2), -MAXOFF, MAXOFF + 1)
    first = jax.random.randint(jax.random.fold_in(key, 1), (), 0, DATES)
    step = jax.random.randint(jax.random.fold_in(key, 2), (), 1, DATES)
    second = (first + step) % DATES
    values = values.at[first, 0].set(MAXOFF)
    values = values.at[second, 0].set(-MAXOFF)
    values = values.at[first, 1].set(-MAXOFF)
    values = values.at[second, 1].set(MAXOFF)
    return values.astype(jnp.int32)


def set_ends(values, own_key, smallest, largest):
    place = [jax.random.randint(jax.random.fold_in(own_key, axis), (), 0, length) for axis, length in enumerate(values.shape)]
    longest = values.shape.index(max(values.shape))
    next_to = place[:longest] + [(place[longest] + 1) % values.shape[longest]] + place[longest + 1:]
    return values.at[tuple(place)].set(smallest).at[tuple(next_to)].set(largest)


def block_scale(rng, shape, pieces, low, top_value):
    level, own = 1.0, jax.random.fold_in(rng, 6)
    for dim, blocks in pieces:
        draws = jnp.exp(jax.random.uniform(jax.random.fold_in(own, dim), (blocks,), jnp.float32, low / len(pieces), top_value / len(pieces)))
        level = level * jnp.repeat(draws, shape[dim] // blocks).reshape([-1 if axis == dim else 1 for axis in range(len(shape))])
    return level


def normal_values(stream_key, shape, deviation, limit, shards=(), held_as=jnp.bfloat16):
    drawn = jax.random.normal(stream_key, shape, jnp.float32) * deviation
    if len(shards) > 0:
        drawn = block_scale(stream_key, shape, shards, -0.22, 0.18) * drawn
    return jnp.clip(drawn, min=-limit, max=limit).astype(held_as)


def setup_inputs(seed: int = 0) -> dict:
    key_list = jax.random.split(jax.random.key(seed), 6)
    slc = normal_values(key_list[0], (DATES, 2, WROWS, COLS), 1.0, 6.0, ((0, 128), (2, 2)))
    coarse = draw_coarse(jax.random.fold_in(key_list[5], 71), 0)
    fraction = set_ends(jax.random.randint(key_list[2], (DATES, 2), 0, NFRAC), jax.random.fold_in(key_list[2], 1), 0, NFRAC - 1).astype(jnp.int32)
    pair_on = set_ends((jax.random.randint(key_list[3], (DATES, SPAN), 0, 3) < 2).astype(jnp.int32), jax.random.fold_in(key_list[3], 1), 0, 1)
    ref_date = jax.random.randint(key_list[4], (1,), 0, DATES).astype(jnp.int32)
    return dict(slc=slc, coarse=coarse, fraction=fraction, pair_on=pair_on, ref_date=ref_date)


col_margin = 64
epsilon = 1e-06

def filter_taps(index):
    position = jnp.arange(8, dtype=jnp.float32) - 3.0 - index.astype(jnp.float32) / NFRAC
    weights = jnp.sinc(position) * (0.54 + 0.46 * jnp.cos(jnp.pi * position / 4.0))
    return (weights / jnp.sum(weights)).astype(jnp.bfloat16)

def multilook(values):
    row_count, col_count = (values.shape[-2], values.shape[-1])
    shaped = values.reshape(values.shape[:-2] + (row_count // LOOK_R, LOOK_R, col_count // LOOK_C, LOOK_C))
    return lax.optimization_barrier(jnp.mean(shaped, axis=(-3, -1)))

def resample(image, offsets, fraction):
    row_taps = filter_taps(fraction[0]).astype(jnp.float32)
    col_taps = filter_taps(fraction[1]).astype(jnp.float32)
    padded = jnp.pad(image.astype(jnp.float32), ((0, 0), (HALO, HALO), (0, 0)))
    total = jnp.zeros((2, WROWS, COLS), jnp.float32)
    for k in range(8):
        start = (HALO + offsets[0] + k - 3).astype(jnp.int32)
        total = total + row_taps[k] * lax.dynamic_slice_in_dim(padded, start, WROWS, 1)
    rowfit = total.astype(jnp.bfloat16)
    padded = jnp.pad(rowfit.astype(jnp.float32), ((0, 0), (0, 0), (col_margin, col_margin)))
    total = jnp.zeros((2, WROWS, COLS), jnp.float32)
    for k in range(8):
        start = (col_margin + offsets[1] + k - 3).astype(jnp.int32)
        total = total + col_taps[k] * lax.dynamic_slice_in_dim(padded, start, COLS, 2)
    return total.astype(jnp.bfloat16)

def pair_terms(first, second):
    z_real, z_imag = (first[0].astype(jnp.float32), first[1].astype(jnp.float32))
    v_real, v_imag = (second[0].astype(jnp.float32), second[1].astype(jnp.float32))
    real_part = multilook(z_real * v_real + z_imag * v_imag)
    imag_part = multilook(z_imag * v_real - z_real * v_imag)
    power_one = multilook(z_real * z_real + z_imag * z_imag)
    power_two = multilook(v_real * v_real + v_imag * v_imag)
    coherent = jnp.sqrt(real_part * real_part + imag_part * imag_part) / (jnp.sqrt(power_one + epsilon) * jnp.sqrt(power_two + epsilon))
    return (jnp.stack([real_part, imag_part]), coherent)

def reference(slc, coarse, fraction, pair_on, ref_date):
    resampled = lax.map(lambda item: resample(item[0], item[1], item[2]), (slc, coarse, fraction))
    ref_image = lax.dynamic_index_in_dim(slc, ref_date[0].astype(jnp.int32), 0, keepdims=False).astype(jnp.float32)

    def with_reference(image):
        z_real, z_imag = (image[0].astype(jnp.float32), image[1].astype(jnp.float32))
        real_part = multilook(z_real * ref_image[0] + z_imag * ref_image[1])
        imag_part = multilook(z_imag * ref_image[0] - z_real * ref_image[1])
        return jnp.stack([real_part, imag_part])
    ref_ifg = lax.map(with_reference, resampled)

    def one_date(item):
        date_index, switches, image = item
        ifg_list, coh_list = ([], [])
        for s in range(SPAN):
            partner = date_index + s + 1
            other = lax.dynamic_index_in_dim(resampled, jnp.minimum(partner, DATES - 1).astype(jnp.int32), 0, keepdims=False)
            usable = jnp.logical_and(partner < DATES, switches[s] == 1)
            ifg, coherent = pair_terms(image, other)
            ifg_list.append(jnp.where(usable, ifg, 0.0))
            coh_list.append(jnp.where(usable, coherent, 0.0))
        return (jnp.stack(ifg_list), jnp.stack(coh_list))
    pair_ifg, coherence = lax.map(one_date, (jnp.arange(DATES, dtype=jnp.int32), pair_on, resampled))
    return (ref_ifg, pair_ifg, coherence)
```

```python
import functools

import jax
import jax.numpy as jnp
import ml_dtypes
import numpy as np
from jax import lax
from jax.experimental import pallas as pl
from jax.experimental.pallas import tpu as pltpu
from jax.sharding import Mesh, PartitionSpec as P

NFRAC = 64
LOOK_R = 5
LOOK_C = 20
EPS = 1e-06
MARGIN = 128
BLK = 256
HALO = 16
BF = jnp.bfloat16
F32 = jnp.float32

GRID = (2, 8, 4, 2)
DATE = ("xl", "z", "y", "core")
FAR = ("xl", "z")


def tap_table():
    x = np.arange(8)[None, :] - 3.0 - np.arange(NFRAC)[:, None] / NFRAC
    w = np.sinc(x) * (0.54 + 0.46 * np.cos(np.pi * x / 4.0))
    taps = (w / w.sum(axis=1, keepdims=True)).astype(np.float32)
    return taps.astype(ml_dtypes.bfloat16).astype(np.float32)


def iota(shape, dim):
    return lax.broadcasted_iota(jnp.int32, shape, dim)


def dot(a, b):
    return jnp.dot(a, b, preferred_element_type=F32)


def source_row(position, groups):
    return (position % groups) * LOOK_R + position // groups


def band(distance, shift, table, index):
    total = jnp.zeros(distance.shape, F32)
    for k in range(8):
        total = jnp.where(distance == shift + k, table[index, k], total)
    return total.astype(BF)


def resample_kernel(meta, table, x, halo, z, fit):
    rows, cols = x.shape[1], x.shape[2]
    groups = rows // LOOK_R
    shift = meta[0] - 3
    out_row = source_row(iota((rows, rows), 0), groups)
    near = band(iota((rows, rows), 1) - out_row, shift, table, meta[2])
    out_row = source_row(iota((rows, HALO), 0), groups)
    start = jnp.where(meta[4] == 0, rows, -HALO)
    edge = band(iota((rows, HALO), 1) + start - out_row, shift, table, meta[2])
    fit[:, :MARGIN] = jnp.zeros((2 * rows, MARGIN), BF)
    fit[:, MARGIN + cols :] = jnp.zeros((2 * rows, MARGIN), BF)
    for p in range(2):
        for c in range(0, cols, BLK):
            fit[p * rows : (p + 1) * rows, MARGIN + c : MARGIN + c + BLK] = (
                dot(near, x[p, :, c : c + BLK]) + dot(edge, halo[p, :, c : c + BLK])
            ).astype(BF)
    span = BLK + 2 * MARGIN
    lanes = iota((span, BLK), 0) - MARGIN - iota((span, BLK), 1)
    taps = band(lanes, meta[1] - 3, table, meta[3])
    for c in range(0, cols, BLK):
        part = dot(fit[:, c : c + span], taps).astype(BF)
        z[0, :, c : c + BLK] = part[:rows]
        z[1, :, c : c + BLK] = part[rows:]


def look_matrix(start, count):
    distance = iota((count, 128), 0) + start - LOOK_C * iota((count, 128), 1)
    return jnp.where((distance >= 0) & (distance < LOOK_C), 1.0, 0.0).astype(BF)


def split_dot(sums, looks):
    high = sums.astype(BF)
    low = (sums - high.astype(F32)).astype(BF)
    return dot(high, looks) + dot(low, looks)


def cross(first, second):
    return (
        first[0] * second[0] + first[1] * second[1],
        first[1] * second[0] - first[0] * second[1],
    )


def power(value):
    return value[0] * value[0] + value[1] * value[1]


def pair_kernel(meta, z, v1, vb, vc, own, back_b, back_c):
    rows, cols = z.shape[1], z.shape[2]
    groups = rows // LOOK_R
    total = jnp.zeros((12 * groups, 128), F32)
    for c in range(0, cols, BLK):
        sums = None
        for j in range(LOOK_R):
            at = slice(j * groups, (j + 1) * groups), slice(c, c + BLK)
            images = [
                (ref[(0,) + at].astype(F32), ref[(1,) + at].astype(F32))
                for ref in (z, v1, vb, vc)
            ]
            a, b, d, e = images
            terms = (
                cross(a, b) + cross(a, d) + cross(a, e) + cross(d, b)
                + (power(a), power(b), power(d), power(e))
            )
            sums = terms if sums is None else [s + t for s, t in zip(sums, terms)]
        total = total + split_dot(jnp.concatenate(sums, axis=0), look_matrix(c, BLK))
    total = total * (1.0 / (LOOK_R * LOOK_C))
    maps = [total[i * groups : (i + 1) * groups] for i in range(12)]
    root = [jnp.sqrt(m + EPS) for m in maps[8:]]
    odd = meta[5] == 1

    def write(out, at, pair, first, second, flip):
        re, im = maps[2 * pair], maps[2 * pair + 1]
        out[at] = re
        out[at + 1] = jnp.where(flip, -im, im)
        out[at + 2] = jnp.sqrt(re * re + im * im) / (root[first] * root[second])

    write(own, 0, 0, 0, 1, False)
    write(own, 3, 1, 0, 2, False)
    write(back_b, 0, 1, 0, 2, odd)
    write(back_b, 3, 3, 2, 1, False)
    write(back_c, 0, 2, 0, 3, odd)


def reference_kernel(meta, z, q_own, q_other, out):
    rows, cols = z.shape[1], z.shape[2]
    groups = rows // LOOK_R
    first = meta[5] == 0
    total = jnp.zeros((2 * groups, 128), F32)
    for c in range(0, cols, 128):
        sums = None
        for j in range(LOOK_R):
            at = slice(j * groups, (j + 1) * groups), slice(c, c + 128)
            start = c // 128 * rows + j * groups
            mine = q_own[start : start + groups].astype(F32)
            other = q_other[start : start + groups].astype(F32)
            a = (z[(0,) + at].astype(F32), z[(1,) + at].astype(F32))
            q = jnp.where(first, mine, other), jnp.where(first, other, mine)
            terms = cross(a, q)
            sums = terms if sums is None else [s + t for s, t in zip(sums, terms)]
        total = total + split_dot(jnp.concatenate(sums, axis=0), look_matrix(c, 128))
    total = total * (1.0 / (LOOK_R * LOOK_C))
    out[0, 0] = total[:groups]
    out[0, 1] = total[groups:]


def candidate_kernel(meta, x, received, out):
    rows, cols = x.shape[1], x.shape[2]
    groups = rows // LOOK_R
    keep = meta[5] == meta[6]
    order = source_row(iota((rows, rows), 0), groups) == iota((rows, rows), 1)
    order = jnp.where(order, 1.0, 0.0).astype(BF)
    for c in range(0, cols, 128):
        mine = x[meta[5], :, c : c + 128]
        value = jnp.where(keep, mine, received[:, c : c + 128])
        out[c // 128 * rows : (c // 128 + 1) * rows] = dot(order, value).astype(BF)
    used = cols // 128 * rows
    out[used:] = jnp.zeros((out.shape[0] - used, 128), BF)


def finish_kernel(meta, on, own, got_b, got_c, ifg, coh):
    odd = meta[5] == 1
    for s in range(3):
        usable = (on[0, s] == 1) & (meta[7] + s + 1 < meta[8])
        for m in range(3):
            if s == 0:
                value = own[m]
            elif s == 1:
                value = jnp.where(odd, got_b[m], own[3 + m])
            else:
                value = jnp.where(odd, got_b[3 + m], got_c[m])
            value = jnp.where(usable, value, 0.0)
            if m < 2:
                ifg[0, s, m] = value
            else:
                coh[0, s] = value


SMEM = pl.BlockSpec(memory_space=pltpu.SMEM)
VMEM = pl.BlockSpec(memory_space=pltpu.VMEM)


def call(kernel, scalars, arrays, outs, flops, scratch=(), size=None):
    moved = sum(a.size * a.dtype.itemsize for a in arrays)
    out_shape = [jax.ShapeDtypeStruct(s, d) for s, d in outs]
    single = len(out_shape) == 1
    return pl.pallas_call(
        kernel,
        out_shape=out_shape[0] if single else out_shape,
        in_specs=[SMEM] * len(scalars) + [VMEM] * len(arrays),
        out_specs=VMEM if single else [VMEM] * len(out_shape),
        scratch_shapes=list(scratch),
        compiler_params=pltpu.CompilerParams(vmem_limit_bytes=32 * 2**20),
        cost_estimate=pl.CostEstimate(flops=flops, bytes_accessed=moved, transcendentals=0),
    )(*scalars, *arrays)


def on_device(table, slc, coarse, fraction, pair_on, ref_date):
    x = slc[0]
    _, rows, cols = x.shape
    groups = rows // LOOK_R
    row = lax.axis_index("row")
    core = lax.axis_index("core")
    date = lax.axis_index(DATE)
    dates = lax.axis_size(DATE)
    near = lax.axis_size("y") * lax.axis_size("core")
    far = dates // near
    ref = ref_date[0]
    meta = jnp.stack(
        [coarse[0, 0], coarse[0, 1], fraction[0, 0], fraction[0, 1], row, core, ref % 2, date, dates]
    ).astype(jnp.int32)

    other = lax.dynamic_index_in_dim(x, 1 - core, 0, keepdims=False)
    other = lax.ppermute(other, "core", [(0, 1), (1, 0)])
    edge = jnp.where(row == 0, x[:, rows - HALO :], x[:, :HALO])
    halo = lax.ppermute(edge, "row", [(0, 1), (1, 0)])

    tiles = cols // 128 * rows
    piece = -(-tiles // (16 * far)) * 16
    cand = call(
        candidate_kernel, [meta], [x, other], [((far * piece, 128), BF)], 2 * rows * rows * cols
    ).reshape(far, piece, 128)

    z = call(
        resample_kernel, [meta, table], [x, halo], [(x.shape, BF)],
        4 * rows * cols * (rows + HALO + BLK + 2 * MARGIN),
        [pltpu.VMEM((2 * rows, cols + 2 * MARGIN), BF)],
    )

    v1 = lax.ppermute(z, DATE, [(i + 1, i) for i in range(dates - 1)])
    pairs_b = [(i, i - 2) for i in range(2, dates, 2)] + [(i, i + 2) for i in range(1, dates - 2, 2)]
    vb = lax.ppermute(z, DATE, pairs_b)
    vc = lax.ppermute(z, DATE, [(i, i + 3) for i in range(0, dates - 3, 2)])

    got = lax.all_to_all(cand, FAR, 0, 0)
    got = lax.dynamic_index_in_dim(got, ref // near, 0)
    got = lax.all_to_all(jnp.broadcast_to(got, (near // 2, piece, 128)), "y", 0, 0)
    got = lax.dynamic_index_in_dim(got, ref % near // 2, 0)
    q_own = lax.all_to_all(jnp.broadcast_to(got, (far, piece, 128)), FAR, 0, 0)
    q_own = q_own.reshape(far * piece, 128)
    q_other = lax.ppermute(q_own, "core", [(0, 1), (1, 0)])

    small = (groups, 128)
    own, back_b, back_c = call(
        pair_kernel, [meta], [z, v1, vb, vc],
        [((6,) + small, F32), ((6,) + small, F32), ((3,) + small, F32)],
        100 * rows * cols,
    )
    got_b = lax.ppermute(back_b, DATE, [(i, i - 2) for i in range(3, dates, 2)])
    got_c = lax.ppermute(back_c, DATE, [(i, i - 3) for i in range(3, dates, 2)])
    ref_ifg = call(
        reference_kernel, [meta], [z, q_own, q_other], [((1, 2) + small, F32)], 30 * rows * cols
    )
    pair_ifg, coherence = call(
        finish_kernel, [meta, pair_on], [own, got_b, got_c],
        [((1, 3, 2) + small, F32), ((1, 3) + small, F32)], 1000,
    )
    return (ref_ifg, pair_ifg, coherence)


def solution(mesh):
    shape = GRID + (mesh.shape["row"],)
    grid = Mesh(mesh.devices.reshape(shape), DATE + ("row",))
    table = tap_table()

    def program(slc, coarse, fraction, pair_on, ref_date):
        return jax.shard_map(
            on_device,
            mesh=grid,
            in_specs=(
                P(),
                P(DATE, None, "row", None),
                P(DATE, None),
                P(DATE, None),
                P(DATE, None),
                P(),
            ),
            out_specs=(
                P(DATE, None, "row", None),
                P(DATE, None, None, "row", None),
                P(DATE, None, "row", None),
            ),
            check_vma=False,
        )(jnp.asarray(table), slc, coarse, fraction, pair_on, ref_date)

    return program
```

```python
import functools

import jax
import jax.numpy as jnp
import ml_dtypes
import numpy as np
from jax import lax
from jax.experimental import pallas as pl
from jax.experimental.pallas import tpu as pltpu
from jax.sharding import Mesh, PartitionSpec as P

NFRAC = 64
LOOK_R = 5
LOOK_C = 20
EPS = 1e-06
MARGIN = 128
BLK = 256
HALO = 16
BF = jnp.bfloat16
F32 = jnp.float32

GRID = (2, 8, 4, 2)
DATE = ("xl", "z", "y", "core")
CHIP = ("xl", "z", "y")


def tap_table():
    x = np.arange(8)[None, :] - 3.0 - np.arange(NFRAC)[:, None] / NFRAC
    w = np.sinc(x) * (0.54 + 0.46 * np.cos(np.pi * x / 4.0))
    taps = (w / w.sum(axis=1, keepdims=True)).astype(np.float32)
    return taps.astype(ml_dtypes.bfloat16).astype(np.float32)


def iota(shape, dim):
    return lax.broadcasted_iota(jnp.int32, shape, dim)


def dot(a, b):
    return jnp.dot(a, b, preferred_element_type=F32)


def source_row(position, groups):
    return (position % groups) * LOOK_R + position // groups


def band(distance, shift, table, index):
    total = jnp.zeros(distance.shape, F32)
    for k in range(8):
        total = jnp.where(distance == shift + k, table[index, k], total)
    return total.astype(BF)


def resample_kernel(coarse, fraction, table, x, halo, z, fit):
    rows, cols = x.shape[1], x.shape[2]
    groups = rows // LOOK_R
    shift = coarse[0, 0] - 3
    out_row = source_row(iota((rows, rows), 0), groups)
    near = band(iota((rows, rows), 1) - out_row, shift, table, fraction[0, 0])
    out_row = source_row(iota((rows, HALO), 0), groups)
    start = jnp.where(lax.axis_index("row") == 0, rows, -HALO)
    edge = band(iota((rows, HALO), 1) + start - out_row, shift, table, fraction[0, 0])
    fit[:, :MARGIN] = jnp.zeros((2 * rows, MARGIN), BF)
    fit[:, MARGIN + cols :] = jnp.zeros((2 * rows, MARGIN), BF)
    for p in range(2):
        for c in range(0, cols, BLK):
            fit[p * rows : (p + 1) * rows, MARGIN + c : MARGIN + c + BLK] = (
                dot(near, x[p, :, c : c + BLK]) + dot(edge, halo[p, :, c : c + BLK])
            ).astype(BF)
    span = BLK + 2 * MARGIN
    lanes = iota((span, BLK), 0) - MARGIN - iota((span, BLK), 1)
    taps = band(lanes, coarse[0, 1] - 3, table, fraction[0, 1])
    for c in range(0, cols, BLK):
        part = dot(fit[:, c : c + span], taps).astype(BF)
        z[0, :, c : c + BLK] = part[:rows]
        z[1, :, c : c + BLK] = part[rows:]


def look_matrix(start, count):
    distance = iota((count, 128), 0) + start - LOOK_C * iota((count, 128), 1)
    return jnp.where((distance >= 0) & (distance < LOOK_C), 1.0, 0.0).astype(BF)


def split_dot(sums, looks):
    high = sums.astype(BF)
    low = (sums - high.astype(F32)).astype(BF)
    return dot(high, looks) + dot(low, looks)


def cross(first, second):
    return (
        first[0] * second[0] + first[1] * second[1],
        first[1] * second[0] - first[0] * second[1],
    )


def power(value):
    return value[0] * value[0] + value[1] * value[1]


def pair_kernel(z, v1, vb, vc, own, back_b, back_c):
    rows, cols = z.shape[1], z.shape[2]
    groups = rows // LOOK_R
    total = jnp.zeros((12 * groups, 128), F32)
    for c in range(0, cols, BLK):
        sums = None
        for j in range(LOOK_R):
            at = slice(j * groups, (j + 1) * groups), slice(c, c + BLK)
            images = [
                (ref[(0,) + at].astype(F32), ref[(1,) + at].astype(F32))
                for ref in (z, v1, vb, vc)
            ]
            a, b, d, e = images
            terms = (
                cross(a, b) + cross(a, d) + cross(a, e) + cross(d, b)
                + (power(a), power(b), power(d), power(e))
            )
            sums = terms if sums is None else [s + t for s, t in zip(sums, terms)]
        total = total + split_dot(jnp.concatenate(sums, axis=0), look_matrix(c, BLK))
    total = total * (1.0 / (LOOK_R * LOOK_C))
    maps = [total[i * groups : (i + 1) * groups] for i in range(12)]
    root = [jnp.sqrt(m + EPS) for m in maps[8:]]
    odd = lax.axis_index("core") == 1

    def write(out, at, pair, first, second, flip):
        re, im = maps[2 * pair], maps[2 * pair + 1]
        out[at] = re
        out[at + 1] = jnp.where(flip, -im, im)
        out[at + 2] = jnp.sqrt(re * re + im * im) / (root[first] * root[second])

    write(own, 0, 0, 0, 1, False)
    write(own, 3, 1, 0, 2, False)
    write(back_b, 0, 1, 0, 2, odd)
    write(back_b, 3, 3, 2, 1, False)
    write(back_c, 0, 2, 0, 3, odd)


def reference_kernel(z, q_own, q_other, out):
    rows, cols = z.shape[1], z.shape[2]
    groups = rows // LOOK_R
    first = lax.axis_index("core") == 0
    total = jnp.zeros((2 * groups, 128), F32)
    for c in range(0, cols, 128):
        sums = None
        for j in range(LOOK_R):
            at = slice(j * groups, (j + 1) * groups), slice(c, c + 128)
            start = c // 128 * rows + j * groups
            mine = q_own[start : start + groups].astype(F32)
            other = q_other[start : start + groups].astype(F32)
            a = (z[(0,) + at].astype(F32), z[(1,) + at].astype(F32))
            q = jnp.where(first, mine, other), jnp.where(first, other, mine)
            terms = cross(a, q)
            sums = terms if sums is None else [s + t for s, t in zip(sums, terms)]
        total = total + split_dot(jnp.concatenate(sums, axis=0), look_matrix(c, 128))
    total = total * (1.0 / (LOOK_R * LOOK_C))
    out[0, 0] = total[:groups]
    out[0, 1] = total[groups:]


def candidate_kernel(ref, x, received, out):
    rows, cols = x.shape[1], x.shape[2]
    groups = rows // LOOK_R
    core = lax.axis_index("core")
    keep = core == ref[0] % 2
    order = source_row(iota((rows, rows), 0), groups) == iota((rows, rows), 1)
    order = jnp.where(order, 1.0, 0.0).astype(BF)
    for c in range(0, cols, 128):
        mine = x[core, :, c : c + 128]
        value = jnp.where(keep, mine, received[:, c : c + 128])
        out[c // 128 * rows : (c // 128 + 1) * rows] = dot(order, value).astype(BF)
    used = cols // 128 * rows
    out[used:] = jnp.zeros((out.shape[0] - used, 128), BF)


def finish_kernel(on, own, got_b, got_c, ifg, coh):
    date, dates = lax.axis_index(DATE), lax.axis_size(DATE)
    odd = lax.axis_index("core") == 1
    for s in range(3):
        usable = (on[0, s] == 1) & (date + s + 1 < dates)
        for m in range(3):
            if s == 0:
                value = own[m]
            elif s == 1:
                value = jnp.where(odd, got_b[m], own[3 + m])
            else:
                value = jnp.where(odd, got_b[3 + m], got_c[m])
            value = jnp.where(usable, value, 0.0)
            if m < 2:
                ifg[0, s, m] = value
            else:
                coh[0, s] = value


SMEM = pl.BlockSpec(memory_space=pltpu.SMEM)
VMEM = pl.BlockSpec(memory_space=pltpu.VMEM)


def call(kernel, scalars, arrays, outs, flops, scratch=(), size=None):
    moved = sum(a.size * a.dtype.itemsize for a in arrays)
    out_shape = [jax.ShapeDtypeStruct(s, d) for s, d in outs]
    single = len(out_shape) == 1
    return pl.pallas_call(
        kernel,
        out_shape=out_shape[0] if single else out_shape,
        in_specs=[SMEM] * len(scalars) + [VMEM] * len(arrays),
        out_specs=VMEM if single else [VMEM] * len(out_shape),
        scratch_shapes=list(scratch),
        compiler_params=pltpu.CompilerParams(vmem_limit_bytes=32 * 2**20),
        cost_estimate=pl.CostEstimate(flops=flops, bytes_accessed=moved, transcendentals=0),
    )(*scalars, *arrays)


def on_device(table, slc, coarse, fraction, pair_on, ref_date):
    x = slc[0]
    _, rows, cols = x.shape
    groups = rows // LOOK_R
    row = lax.axis_index("row")
    core = lax.axis_index("core")
    dates = lax.axis_size(DATE)
    chips = dates // lax.axis_size("core")
    ref = ref_date[0]
    other = lax.dynamic_index_in_dim(x, 1 - core, 0, keepdims=False)
    other = lax.ppermute(other, "core", [(0, 1), (1, 0)])
    edge = jnp.where(row == 0, x[:, rows - HALO :], x[:, :HALO])
    halo = lax.ppermute(edge, "row", [(0, 1), (1, 0)])

    tiles = cols // 128 * rows
    piece = -(-tiles // (16 * chips)) * 16
    cand = call(
        candidate_kernel, [ref_date], [x, other], [((chips * piece, 128), BF)], 2 * rows * rows * cols
    ).reshape(chips, piece, 128)

    z = call(
        resample_kernel, [coarse, fraction, table], [x, halo], [(x.shape, BF)],
        4 * rows * cols * (rows + HALO + BLK + 2 * MARGIN),
        [pltpu.VMEM((2 * rows, cols + 2 * MARGIN), BF)],
    )

    got = lax.all_to_all(cand, CHIP, 0, 0)
    got, z = lax.optimization_barrier((got, z))
    got = lax.dynamic_index_in_dim(got, ref // 2, 0)
    q_own = lax.all_to_all(jnp.broadcast_to(got, (chips, piece, 128)), CHIP, 0, 0)
    q_own = q_own.reshape(chips * piece, 128)
    q_other = lax.ppermute(q_own, "core", [(0, 1), (1, 0)])

    v1 = lax.ppermute(z, DATE, [(i + 1, i) for i in range(dates - 1)])
    pairs_b = [(i, i - 2) for i in range(2, dates, 2)] + [(i, i + 2) for i in range(1, dates - 2, 2)]
    vb = lax.ppermute(z, DATE, pairs_b)
    vc = lax.ppermute(z, DATE, [(i, i + 3) for i in range(0, dates - 3, 2)])

    small = (groups, 128)
    own, back_b, back_c = call(
        pair_kernel, [], [z, v1, vb, vc],
        [((6,) + small, F32), ((6,) + small, F32), ((3,) + small, F32)],
        100 * rows * cols,
    )
    got_b = lax.ppermute(back_b, DATE, [(i, i - 2) for i in range(3, dates, 2)])
    got_c = lax.ppermute(back_c, DATE, [(i, i - 3) for i in range(3, dates, 2)])
    ref_ifg = call(
        reference_kernel, [], [z, q_own, q_other], [((1, 2) + small, F32)], 30 * rows * cols
    )
    pair_ifg, coherence = call(
        finish_kernel, [pair_on], [own, got_b, got_c],
        [((1, 3, 2) + small, F32), ((1, 3) + small, F32)], 1000,
    )
    return (ref_ifg, pair_ifg, coherence)


def solution(mesh):
    shape = GRID + (mesh.shape["row"],)
    grid = Mesh(mesh.devices.reshape(shape), DATE + ("row",))
    table = tap_table()

    def program(slc, coarse, fraction, pair_on, ref_date):
        return jax.shard_map(
            on_device,
            mesh=grid,
            in_specs=(
                P(),
                P(DATE, None, "row", None),
                P(DATE, None),
                P(DATE, None),
                P(DATE, None),
                P(),
            ),
            out_specs=(
                P(DATE, None, "row", None),
                P(DATE, None, None, "row", None),
                P(DATE, None, "row", None),
            ),
            check_vma=False,
        )(jnp.asarray(table), slc, coarse, fraction, pair_on, ref_date)

    return program
```

```python
import jax
import jax.numpy as jnp
import ml_dtypes
import numpy as np
from jax import lax
from jax.experimental import pallas as pl
from jax.experimental.pallas import tpu as pltpu
from jax.sharding import Mesh, PartitionSpec as P

NFRAC = 64
SPAN = 3
LOOK_R = 5
LOOK_C = 20
EPS = 1e-06
BF = jnp.bfloat16
F32 = jnp.float32

GRID = (2, 8, 4, 2)
DATE = ("xl", "z", "y", "core")
FAR = ("xl", "z")
NEAR = ("y", "core", "row")

SLAB = 160
WIN = 192
LEAD = 16
LANES = 2 * WIN
SPARE = 190
SLOT = SLAB // LOOK_C


def tap_table():
    x = np.arange(8)[None, :] - 3.0 - np.arange(NFRAC)[:, None] / NFRAC
    w = np.sinc(x) * (0.54 + 0.46 * np.cos(np.pi * x / 4.0))
    taps = (w / w.sum(axis=1, keepdims=True)).astype(np.float32)
    return taps.astype(ml_dtypes.bfloat16).astype(np.float32)


def iota(shape, dim):
    return lax.broadcasted_iota(jnp.int32, shape, dim)


def dot(a, b):
    return jnp.dot(a, b, preferred_element_type=F32)


def row_distance(rows):
    looks = rows // LOOK_R
    out = iota((rows, rows), 0)
    return iota((rows, rows), 1) - (out % looks) * LOOK_R - out // looks


def lane_distance():
    return iota((256, 128), 0) - iota((256, 128), 1)


def band(distance, shift, table, index):
    total = jnp.zeros(distance.shape, F32)
    for k in range(8):
        total = jnp.where(distance == shift + k, table[index, k], total)
    return total.astype(BF)


def filtered(image, row_band, lane_band):
    fit = dot(row_band, image).astype(BF)
    return jnp.concatenate(
        [
            dot(fit[:, :256], lane_band),
            dot(fit[:, 128:], lane_band),
            dot(fit[:, 256:], lane_band[:128]),
        ],
        axis=1,
    )


def crossed(value):
    turned = pltpu.roll(value, WIN, 1)
    return jnp.where(iota(value.shape, 1) < WIN, -turned, turned)


def look_matrix():
    lane = iota((LANES, 128), 0)
    col = jnp.where(lane < WIN, lane, lane - WIN)
    distance = col - LOOK_C * iota((LANES, 128), 1)
    inside = (col < SLAB) & (distance >= 0) & (distance < LOOK_C)
    return jnp.where(inside, 1.0, 0.0).astype(BF)


def looks_of(sums, looks):
    high = sums.astype(BF)
    low = (sums - high.astype(F32)).astype(BF)
    return dot(high, looks) + dot(low, looks)


def row_sum(first, second):
    rows = first.shape[0] // LOOK_R
    total = None
    for j in range(LOOK_R):
        part = first[j * rows : (j + 1) * rows].astype(F32) * second[j * rows : (j + 1) * rows].astype(F32)
        total = part if total is None else total + part
    return total


def pack_kernel(coarse, fraction, x, out, wide):
    _, rows, cols = x.shape
    for p in range(2):
        wide[p, :, :128] = jnp.zeros((rows, 128), BF)
        wide[p, :, 128 + cols :] = jnp.zeros((rows, 128), BF)
        wide[p, :, 128 : 128 + cols] = x[p]
    lane = iota((rows, LANES), 1)
    row = iota((rows, LANES), 0)
    own = jnp.where(row == 0, coarse[0, 0], jnp.where(row == 1, coarse[0, 1], 0))
    own = jnp.where(row == 2, fraction[0, 0], jnp.where(row == 3, fraction[0, 1], own))
    own = own.astype(F32)
    for j in range(out.shape[0]):
        start = 128 + SLAB * j - LEAD
        base, off = start // 128 * 128, start % 128
        first = pltpu.roll(wide[0, :, base : base + LANES].astype(F32), (LANES - off) % LANES, 1)
        second = pltpu.roll(wide[1, :, base : base + LANES].astype(F32), WIN - off, 1)
        value = jnp.where(lane < WIN, first, second)
        out[j] = jnp.where(lane == SPARE, own, value).astype(BF)


def candidate_kernel(image, out):
    rows = image.shape[0]
    order = jnp.where(row_distance(rows) == 0, 1.0, 0.0).astype(BF)
    shift = jnp.where(lane_distance() == LEAD, 1.0, 0.0).astype(BF)
    value = filtered(image[...], order, shift).astype(BF)
    for t in range(LANES // 128):
        out[t * rows : (t + 1) * rows] = value[:, t * 128 : (t + 1) * 128]
    used = LANES // 128 * rows
    out[used:] = jnp.zeros((out.shape[0] - used, 128), BF)


def pair_kernel(offsets, later_offsets, table, images, later, z, out, turned, powers):
    dates, rows, _ = images.shape
    looks = look_matrix()
    rows_apart, lanes_apart = row_distance(rows), lane_distance()

    def resample(images, offsets, base):
        def step(n, carry):
            row_band = band(rows_apart, offsets[n, 0] - 3, table, offsets[n, 2])
            lane_band = band(lanes_apart, LEAD + offsets[n, 1] - 3, table, offsets[n, 3])
            value = filtered(images[n], row_band, lane_band)
            z[base + n] = value.astype(BF)
            turned[base + n] = crossed(value).astype(BF)
            value = z[base + n]
            powers[base + n] = looks_of(row_sum(value, value), looks)
            return carry

        lax.fori_loop(0, images.shape[0], step, 0)

    resample(images, offsets, 0)
    resample(later, later_offsets, dates)
    count = rows // LOOK_R

    def step(n, carry):
        first = z[n]
        sums = []
        for s in range(SPAN):
            sums.append(row_sum(first, z[n + s + 1]))
            sums.append(row_sum(first, turned[n + s + 1]))
        maps = looks_of(jnp.concatenate(sums, axis=0), looks)
        total = jnp.zeros((count, 128), F32)
        for i in range(2 * SPAN):
            total = total + pltpu.roll(maps[i * count : (i + 1) * count], SLOT * (2 + i), 1)
        for i in range(SPAN + 1):
            total = total + pltpu.roll(powers[n + i], SLOT * (2 + 2 * SPAN + i), 1)
        out[n] = total
        return carry

    lax.fori_loop(0, dates, step, 0)


def reference_kernel(part, z, q, out, first, second):
    dates, count, _ = part.shape
    rows = z.shape[1]
    looks = look_matrix()
    value = jnp.concatenate(
        [q[t * rows : (t + 1) * rows].astype(F32) for t in range(LANES // 128)], axis=1
    )
    first[...] = value.astype(BF)
    second[...] = crossed(value).astype(BF)

    def step(n, carry):
        image = z[n]
        sums = [row_sum(image, first[...]), row_sum(image, second[...])]
        maps = looks_of(jnp.concatenate(sums, axis=0), looks)
        out[n] = part[n] + maps[:count] + pltpu.roll(maps[count:], SLOT, 1)
        return carry

    lax.fori_loop(0, dates, step, 0)


def finish_kernel(on, got, ref_ifg, pair_ifg, coherence):
    slabs, count, _ = got.shape
    date, dates = lax.axis_index(DATE), lax.axis_size(DATE)
    slab = iota((count, 128), 1) // SLOT

    def gathered(m):
        total = jnp.zeros((count, 128), F32)
        for j in range(slabs):
            moved = pltpu.roll(got[j], SLOT * ((j - m) % slabs), 1)
            total = jnp.where(slab == j, moved, total)
        return total * (1.0 / (LOOK_R * LOOK_C))

    ref_ifg[0, 0] = gathered(0)
    ref_ifg[0, 1] = gathered(1)
    own = jnp.sqrt(gathered(2 + 2 * SPAN) + EPS)
    for s in range(SPAN):
        usable = (on[0, s] == 1) & (date + s + 1 < dates)
        re, im = gathered(2 + 2 * s), gathered(3 + 2 * s)
        other = jnp.sqrt(gathered(3 + 2 * SPAN + s) + EPS)
        coh = jnp.sqrt(re * re + im * im) / (own * other)
        pair_ifg[0, s, 0] = jnp.where(usable, re, 0.0)
        pair_ifg[0, s, 1] = jnp.where(usable, im, 0.0)
        coherence[0, s] = jnp.where(usable, coh, 0.0)


SMEM = pl.BlockSpec(memory_space=pltpu.SMEM)
VMEM = pl.BlockSpec(memory_space=pltpu.VMEM)


def call(kernel, scalars, arrays, outs, flops, scratch=()):
    moved = sum(a.size * a.dtype.itemsize for a in arrays)
    out_shape = [jax.ShapeDtypeStruct(s, d) for s, d in outs]
    single = len(out_shape) == 1
    return pl.pallas_call(
        kernel,
        out_shape=out_shape[0] if single else out_shape,
        in_specs=[SMEM] * len(scalars) + [VMEM] * len(arrays),
        out_specs=VMEM if single else [VMEM] * len(out_shape),
        scratch_shapes=list(scratch),
        compiler_params=pltpu.CompilerParams(vmem_limit_bytes=40 * 2**20),
        cost_estimate=pl.CostEstimate(flops=flops, bytes_accessed=moved, transcendentals=0),
    )(*scalars, *arrays)


def on_device(table, slc, coarse, fraction, pair_on, ref_date):
    x = slc[0]
    _, rows, cols = x.shape
    members = lax.axis_size("y") * lax.axis_size("core")
    halves = lax.axis_size("row")
    slabs = members * halves
    groups = lax.axis_size(FAR)
    all_rows = rows * halves
    count = all_rows // LOOK_R
    ref = ref_date[0]

    packed = call(
        pack_kernel, [coarse, fraction], [x], [((slabs, rows, LANES), BF)], 10**8,
        [pltpu.VMEM((2, rows, cols + 256), BF)],
    )
    images = lax.all_to_all(packed, NEAR, 0, 0).reshape(members, all_rows, LANES)

    later = lax.ppermute(images[:SPAN], FAR, [(i + 1, i) for i in range(groups - 1)])

    tiles = LANES // 128 * all_rows
    piece = -(-tiles // (16 * groups)) * 16
    cand = lax.dynamic_index_in_dim(images, ref % members, 0, keepdims=False)
    cand = call(candidate_kernel, [], [cand], [((groups * piece, 128), BF)], 10**8)
    got = lax.all_to_all(cand.reshape(groups, piece, 128), FAR, 0, 0)
    got = lax.dynamic_index_in_dim(got, ref // members, 0)
    q = lax.all_to_all(jnp.broadcast_to(got, (groups, piece, 128)), FAR, 0, 0)
    q = q.reshape(groups * piece, 128)

    offsets = images[:, :4, SPARE].astype(jnp.int32)
    later_offsets = later[:, :4, SPARE].astype(jnp.int32)
    held = (members + SPAN, all_rows, LANES)
    z, part = call(
        pair_kernel, [offsets, later_offsets, table], [images, later],
        [(held, BF), ((members, count, 128), F32)], 4 * 10**9,
        [pltpu.VMEM(held, BF), pltpu.VMEM((members + SPAN, count, 128), F32)],
    )
    maps = call(
        reference_kernel, [], [part, z, q], [((members, count, 128), F32)], 10**9,
        [pltpu.VMEM((all_rows, LANES), BF)] * 2,
    )
    got = lax.all_to_all(maps.reshape(slabs, count // halves, 128), NEAR, 0, 0)
    small = (count // halves, 128)
    return call(
        finish_kernel, [pair_on], [got],
        [((1, 2) + small, F32), ((1, SPAN, 2) + small, F32), ((1, SPAN) + small, F32)], 10**7,
    )


def solution(mesh):
    shape = GRID + (mesh.shape["row"],)
    grid = Mesh(mesh.devices.reshape(shape), DATE + ("row",))
    table = tap_table()

    def program(slc, coarse, fraction, pair_on, ref_date):
        return tuple(
            jax.shard_map(
                on_device,
                mesh=grid,
                in_specs=(
                    P(),
                    P(DATE, None, "row", None),
                    P(DATE, None),
                    P(DATE, None),
                    P(DATE, None),
                    P(),
                ),
                out_specs=(
                    P(DATE, None, "row", None),
                    P(DATE, None, None, "row", None),
                    P(DATE, None, "row", None),
                ),
                check_vma=False,
            )(jnp.asarray(table), slc, coarse, fraction, pair_on, ref_date)
        )

    return program
```

```python
import jax
import jax.numpy as jnp
import ml_dtypes
import numpy as np
from jax import lax
from jax.experimental import pallas as pl
from jax.experimental.pallas import tpu as pltpu
from jax.sharding import Mesh, PartitionSpec as P

NFRAC = 64
SPAN = 3
LOOK_R = 5
LOOK_C = 20
EPS = 1e-06
BF = jnp.bfloat16
F32 = jnp.float32

GRID = (2, 8, 4, 2)
DATE = ("xl", "z", "y", "core")
FAR = ("xl", "z")
NEAR = ("y", "core", "row")

SLAB = 160
WIN = 192
LEAD = 16
LANES = 2 * WIN
SPARE = 190
SLOT = SLAB // LOOK_C


def tap_table():
    x = np.arange(8)[None, :] - 3.0 - np.arange(NFRAC)[:, None] / NFRAC
    w = np.sinc(x) * (0.54 + 0.46 * np.cos(np.pi * x / 4.0))
    taps = (w / w.sum(axis=1, keepdims=True)).astype(np.float32)
    return taps.astype(ml_dtypes.bfloat16).astype(np.float32)


def iota(shape, dim):
    return lax.broadcasted_iota(jnp.int32, shape, dim)


def dot(a, b):
    return jnp.dot(a, b, preferred_element_type=F32)


def row_distance(rows):
    looks = rows // LOOK_R
    out = iota((rows, rows), 0)
    return iota((rows, rows), 1) - (out % looks) * LOOK_R - out // looks


def lane_distance():
    return iota((256, 128), 0) - iota((256, 128), 1)


def band(distance, shift, table, index):
    total = jnp.zeros(distance.shape, F32)
    for k in range(8):
        total = jnp.where(distance == shift + k, table[index, k], total)
    return total.astype(BF)


def filtered(image, row_band, lane_band):
    fit = dot(row_band, image).astype(BF)
    return jnp.concatenate(
        [
            dot(fit[:, :256], lane_band),
            dot(fit[:, 128:], lane_band),
            dot(fit[:, 256:], lane_band[:128]),
        ],
        axis=1,
    )


def crossed(value):
    turned = pltpu.roll(value, WIN, 1)
    return jnp.where(iota(value.shape, 1) < WIN, -turned, turned)


def look_matrix():
    lane = iota((LANES, 128), 0)
    col = jnp.where(lane < WIN, lane, lane - WIN)
    distance = col - LOOK_C * iota((LANES, 128), 1)
    inside = (col < SLAB) & (distance >= 0) & (distance < LOOK_C)
    return jnp.where(inside, 1.0, 0.0).astype(BF)


def looks_of(sums, looks):
    high = sums.astype(BF)
    low = (sums - high.astype(F32)).astype(BF)
    return dot(high, looks) + dot(low, looks)


def row_sum(first, second):
    rows = first.shape[0] // LOOK_R
    total = None
    for j in range(LOOK_R):
        part = first[j * rows : (j + 1) * rows].astype(F32) * second[j * rows : (j + 1) * rows].astype(F32)
        total = part if total is None else total + part
    return total


def pack_kernel(coarse, fraction, x, out, wide, shifts, taps, image_sem, small_sem):
    _, _, rows, cols = x.shape
    copies = [
        pltpu.make_async_copy(x.at[0, p], wide.at[p, :, pl.ds(128, cols)], image_sem.at[p])
        for p in range(2)
    ]
    copies.append(pltpu.make_async_copy(coarse, shifts, small_sem.at[0]))
    copies.append(pltpu.make_async_copy(fraction, taps, small_sem.at[1]))
    for copy in copies:
        copy.start()
    for p in range(2):
        wide[p, :, :128] = jnp.zeros((rows, 128), BF)
        wide[p, :, 128 + cols :] = jnp.zeros((rows, 128), BF)
    lane = iota((rows, LANES), 1)
    row = iota((rows, LANES), 0)
    for copy in copies:
        copy.wait()
    own = jnp.where(row == 0, shifts[0, 0], jnp.where(row == 1, shifts[0, 1], 0))
    own = jnp.where(row == 2, taps[0, 0], jnp.where(row == 3, taps[0, 1], own))
    own = own.astype(F32)
    for j in range(out.shape[0]):
        start = 128 + SLAB * j - LEAD
        base, off = start // 128 * 128, start % 128
        first = pltpu.roll(wide[0, :, base : base + LANES].astype(F32), (LANES - off) % LANES, 1)
        second = pltpu.roll(wide[1, :, base : base + LANES].astype(F32), WIN - off, 1)
        value = jnp.where(lane < WIN, first, second)
        out[j] = jnp.where(lane == SPARE, own, value).astype(BF)


def candidate_kernel(image, out):
    rows = image.shape[0]
    order = jnp.where(row_distance(rows) == 0, 1.0, 0.0).astype(BF)
    shift = jnp.where(lane_distance() == LEAD, 1.0, 0.0).astype(BF)
    value = filtered(image[...], order, shift).astype(BF)
    for t in range(LANES // 128):
        out[t * rows : (t + 1) * rows] = value[:, t * 128 : (t + 1) * 128]
    used = LANES // 128 * rows
    out[used:] = jnp.zeros((out.shape[0] - used, 128), BF)


def resampled(image, offsets, n, table, rows_apart, lanes_apart):
    row_band = band(rows_apart, offsets[n, 0] - 3, table, offsets[n, 2])
    lane_band = band(lanes_apart, LEAD + offsets[n, 1] - 3, table, offsets[n, 3])
    return filtered(image, row_band, lane_band)


def pair_looks(first, partners, looks):
    sums = []
    for _, image, turned, _ in partners:
        sums.append(row_sum(first, image))
        sums.append(row_sum(first, turned))
    maps = looks_of(jnp.concatenate(sums, axis=0), looks)
    count = sums[0].shape[0]
    total = jnp.zeros((count, 128), F32)
    for i, (s, _, _, power) in enumerate(partners):
        for c in range(2):
            one = maps[(2 * i + c) * count : (2 * i + c + 1) * count]
            total = total + pltpu.roll(one, SLOT * (2 + 2 * s + c), 1)
        total = total + pltpu.roll(power, SLOT * (3 + 2 * SPAN + s), 1)
    return total


def own_kernel(offsets, table, images, z, out, turned, powers):
    dates, rows, _ = images.shape
    looks = look_matrix()
    rows_apart, lanes_apart = row_distance(rows), lane_distance()
    for n in range(dates):
        value = resampled(images[n], offsets, n, table, rows_apart, lanes_apart)
        z[n] = value.astype(BF)
        turned[n] = crossed(value).astype(BF)
        powers[n] = looks_of(row_sum(z[n], z[n]), looks)
    for n in range(dates):
        total = pltpu.roll(powers[n], SLOT * (2 + 2 * SPAN), 1)
        spans = [s for s in range(SPAN) if n + s + 1 < dates]
        if spans:
            partners = [(s, z[n + s + 1], turned[n + s + 1], powers[n + s + 1]) for s in spans]
            total = total + pair_looks(z[n], partners, looks)
        out[n] = total


def later_kernel(offsets, table, later, z, out):
    dates, rows, _ = later.shape
    looks = look_matrix()
    rows_apart, lanes_apart = row_distance(rows), lane_distance()
    found = []
    for n in range(dates):
        value = resampled(later[n], offsets, n, table, rows_apart, lanes_apart)
        image = value.astype(BF)
        power = looks_of(row_sum(image, image), looks)
        found.append((image, crossed(value).astype(BF), power))
    for n in range(dates):
        partners = [(m - n + dates - 1,) + found[m] for m in range(n + 1)]
        out[n] = pair_looks(z[n], partners, looks)


def reference_kernel(part, later_part, z, q, out):
    dates = part.shape[0]
    rows = z.shape[1]
    looks = look_matrix()
    value = jnp.concatenate(
        [q[t * rows : (t + 1) * rows].astype(F32) for t in range(LANES // 128)], axis=1
    )
    turned = crossed(value).astype(BF)
    value = value.astype(BF)
    for n in range(dates):
        maps = looks_of(jnp.concatenate([row_sum(z[n], value), row_sum(z[n], turned)], axis=0), looks)
        count = maps.shape[0] // 2
        total = part[n] + maps[:count] + pltpu.roll(maps[count:], SLOT, 1)
        if n >= dates - SPAN:
            total = total + later_part[n - dates + SPAN]
        out[n] = total


def finish_kernel(on, got, ref_ifg, pair_ifg, coherence):
    slabs, count, _ = got.shape
    date, dates = lax.axis_index(DATE), lax.axis_size(DATE)
    slab = iota((count, 128), 1) // SLOT

    def gathered(m):
        total = jnp.zeros((count, 128), F32)
        for j in range(slabs):
            moved = pltpu.roll(got[j], SLOT * ((j - m) % slabs), 1)
            total = jnp.where(slab == j, moved, total)
        return total * (1.0 / (LOOK_R * LOOK_C))

    ref_ifg[0, 0] = gathered(0)
    ref_ifg[0, 1] = gathered(1)
    own = jnp.sqrt(gathered(2 + 2 * SPAN) + EPS)
    for s in range(SPAN):
        usable = (on[0, s] == 1) & (date + s + 1 < dates)
        re, im = gathered(2 + 2 * s), gathered(3 + 2 * s)
        other = jnp.sqrt(gathered(3 + 2 * SPAN + s) + EPS)
        coh = jnp.sqrt(re * re + im * im) / (own * other)
        pair_ifg[0, s, 0] = jnp.where(usable, re, 0.0)
        pair_ifg[0, s, 1] = jnp.where(usable, im, 0.0)
        coherence[0, s] = jnp.where(usable, coh, 0.0)


SMEM = pl.BlockSpec(memory_space=pltpu.SMEM)
VMEM = pl.BlockSpec(memory_space=pltpu.VMEM)


def call(kernel, scalars, arrays, outs, flops, scratch=()):
    moved = sum(a.size * a.dtype.itemsize for a in arrays)
    out_shape = [jax.ShapeDtypeStruct(s, d) for s, d in outs]
    single = len(out_shape) == 1
    return pl.pallas_call(
        kernel,
        out_shape=out_shape[0] if single else out_shape,
        in_specs=[SMEM] * len(scalars) + [VMEM] * len(arrays),
        out_specs=VMEM if single else [VMEM] * len(out_shape),
        scratch_shapes=list(scratch),
        compiler_params=pltpu.CompilerParams(vmem_limit_bytes=40 * 2**20),
        cost_estimate=pl.CostEstimate(flops=flops, bytes_accessed=moved, transcendentals=0),
    )(*scalars, *arrays)


def on_device(table, slc, coarse, fraction, pair_on, ref_date):
    _, _, rows, cols = slc.shape
    members = lax.axis_size("y") * lax.axis_size("core")
    halves = lax.axis_size("row")
    slabs = members * halves
    groups = lax.axis_size(FAR)
    all_rows = rows * halves
    count = all_rows // LOOK_R
    ref = ref_date[0]

    anywhere = pl.BlockSpec(memory_space=pl.ANY)
    packed = pl.pallas_call(
        pack_kernel,
        out_shape=jax.ShapeDtypeStruct((slabs, rows, LANES), BF),
        in_specs=[anywhere] * 3,
        out_specs=VMEM,
        scratch_shapes=[
            pltpu.VMEM((2, rows, cols + 256), BF),
            pltpu.SMEM((1, 2), jnp.int32),
            pltpu.SMEM((1, 2), jnp.int32),
            pltpu.SemaphoreType.DMA((2,)),
            pltpu.SemaphoreType.DMA((2,)),
        ],
        compiler_params=pltpu.CompilerParams(vmem_limit_bytes=60 * 2**20),
        cost_estimate=pl.CostEstimate(flops=10**8, bytes_accessed=2 * 10**6, transcendentals=0),
    )(coarse, fraction, slc)
    images = lax.all_to_all(packed, NEAR, 0, 0).reshape(members, all_rows, LANES)

    tiles = LANES // 128 * all_rows
    piece = -(-tiles // (16 * groups)) * 16
    cand = lax.dynamic_index_in_dim(images, ref % members, 0, keepdims=False)
    cand = call(candidate_kernel, [], [cand], [((groups * piece, 128), BF)], 10**8)
    got = lax.all_to_all(cand.reshape(groups, piece, 128), FAR, 0, 0)
    offsets = images[:, :4, SPARE].astype(jnp.int32)
    z, part = call(
        own_kernel, [offsets, table], [images],
        [(images.shape, BF), ((members, count, 128), F32)], 4 * 10**9,
        [pltpu.VMEM(images.shape, BF), pltpu.VMEM((members, count, 128), F32)],
    )
    got, z = lax.optimization_barrier((got, z))
    later = lax.ppermute(images[:SPAN], FAR, [(i + 1, i) for i in range(groups - 1)])

    got = lax.dynamic_index_in_dim(got, ref // members, 0)
    q = lax.all_to_all(jnp.broadcast_to(got, (groups, piece, 128)), FAR, 0, 0)
    q = q.reshape(groups * piece, 128)

    later_offsets = later[:, :4, SPARE].astype(jnp.int32)
    later_part = call(
        later_kernel, [later_offsets, table], [later, z[members - SPAN :]],
        [((SPAN, count, 128), F32)], 2 * 10**9,
    )
    maps = call(
        reference_kernel, [], [part, later_part, z, q], [((members, count, 128), F32)], 10**9
    )
    got = lax.all_to_all(maps.reshape(slabs, count // halves, 128), NEAR, 0, 0)
    small = (count // halves, 128)
    return call(
        finish_kernel, [pair_on], [got],
        [((1, 2) + small, F32), ((1, SPAN, 2) + small, F32), ((1, SPAN) + small, F32)], 10**7,
    )


def solution(mesh):
    shape = GRID + (mesh.shape["row"],)
    grid = Mesh(mesh.devices.reshape(shape), DATE + ("row",))
    table = tap_table()

    def program(slc, coarse, fraction, pair_on, ref_date):
        return tuple(
            jax.shard_map(
                on_device,
                mesh=grid,
                in_specs=(
                    P(),
                    P(DATE, None, "row", None),
                    P(DATE, None),
                    P(DATE, None),
                    P(DATE, None),
                    P(),
                ),
                out_specs=(
                    P(DATE, None, "row", None),
                    P(DATE, None, None, "row", None),
                    P(DATE, None, "row", None),
                ),
                check_vma=False,
            )(jnp.asarray(table), slc, coarse, fraction, pair_on, ref_date)
        )

    return program
```

```python
import jax
import jax.numpy as jnp
import ml_dtypes
import numpy as np
from jax import lax
from jax.experimental import pallas as pl
from jax.experimental.pallas import tpu as pltpu
from jax.sharding import Mesh, PartitionSpec as P

NFRAC = 64
SPAN = 3
LOOK_R = 5
LOOK_C = 20
EPS = 1e-06
BF = jnp.bfloat16
F32 = jnp.float32

GRID = (2, 8, 4, 2)
DATE = ("xl", "z", "y", "core")
FAR = ("xl", "z")
NEAR = ("y", "core", "row")

SLAB = 160
WIN = 192
LEAD = 16
LANES = 2 * WIN
SPARE = 190
SLOT = SLAB // LOOK_C


def tap_table():
    x = np.arange(8)[None, :] - 3.0 - np.arange(NFRAC)[:, None] / NFRAC
    w = np.sinc(x) * (0.54 + 0.46 * np.cos(np.pi * x / 4.0))
    taps = (w / w.sum(axis=1, keepdims=True)).astype(np.float32)
    return taps.astype(ml_dtypes.bfloat16).astype(np.float32)


def iota(shape, dim):
    return lax.broadcasted_iota(jnp.int32, shape, dim)


def dot(a, b):
    return jnp.dot(a, b, preferred_element_type=F32)


def row_distance(rows):
    looks = rows // LOOK_R
    out = iota((rows, rows), 0)
    return iota((rows, rows), 1) - (out % looks) * LOOK_R - out // looks


def lane_distance():
    return iota((256, 128), 0) - iota((256, 128), 1)


def band(distance, shift, table, index):
    total = jnp.zeros(distance.shape, F32)
    for k in range(8):
        total = jnp.where(distance == shift + k, table[index, k], total)
    return total.astype(BF)


def filtered(image, row_band, lane_band):
    fit = dot(row_band, image).astype(BF)
    return jnp.concatenate(
        [
            dot(fit[:, :256], lane_band),
            dot(fit[:, 128:], lane_band),
            dot(fit[:, 256:], lane_band[:128]),
        ],
        axis=1,
    )


def crossed(value):
    turned = pltpu.roll(value, WIN, 1)
    return jnp.where(iota(value.shape, 1) < WIN, -turned, turned)


def look_matrix():
    lane = iota((LANES, 128), 0)
    col = jnp.where(lane < WIN, lane, lane - WIN)
    distance = col - LOOK_C * iota((LANES, 128), 1)
    inside = (col < SLAB) & (distance >= 0) & (distance < LOOK_C)
    return jnp.where(inside, 1.0, 0.0).astype(BF)


def looks_of(sums, looks):
    high = sums.astype(BF)
    low = (sums - high.astype(F32)).astype(BF)
    return dot(high, looks) + dot(low, looks)


def row_sum(first, second):
    rows = first.shape[0] // LOOK_R
    total = None
    for j in range(LOOK_R):
        part = first[j * rows : (j + 1) * rows].astype(F32) * second[j * rows : (j + 1) * rows].astype(F32)
        total = part if total is None else total + part
    return total


def pack_kernel(coarse, fraction, x, out, wide, shifts, taps, image_sem, small_sem):
    _, _, rows, cols = x.shape
    copies = [
        pltpu.make_async_copy(x.at[0, p], wide.at[p, :, pl.ds(128, cols)], image_sem.at[p])
        for p in range(2)
    ]
    copies.append(pltpu.make_async_copy(coarse, shifts, small_sem.at[0]))
    copies.append(pltpu.make_async_copy(fraction, taps, small_sem.at[1]))
    for copy in copies:
        copy.start()
    for p in range(2):
        wide[p, :, :128] = jnp.zeros((rows, 128), BF)
        wide[p, :, 128 + cols :] = jnp.zeros((rows, 128), BF)
    lane = iota((rows, LANES), 1)
    row = iota((rows, LANES), 0)
    for copy in copies:
        copy.wait()
    own = jnp.where(row == 0, shifts[0, 0], jnp.where(row == 1, shifts[0, 1], 0))
    own = jnp.where(row == 2, taps[0, 0], jnp.where(row == 3, taps[0, 1], own))
    own = own.astype(F32)
    for j in range(out.shape[0]):
        start = 128 + SLAB * j - LEAD
        base, off = start // 128 * 128, start % 128
        first = pltpu.roll(wide[0, :, base : base + LANES].astype(F32), (LANES - off) % LANES, 1)
        second = pltpu.roll(wide[1, :, base : base + LANES].astype(F32), WIN - off, 1)
        value = jnp.where(lane < WIN, first, second)
        out[j] = jnp.where(lane == SPARE, own, value).astype(BF)


def candidate_kernel(image, out):
    rows = image.shape[0]
    half = rows // 2
    order = jnp.where(row_distance(rows) == 0, 1.0, 0.0).astype(BF)
    shift = jnp.where(lane_distance() == LEAD, 1.0, 0.0).astype(BF)
    value = filtered(image[...], order, shift)
    lane = iota((rows, 128), 1)
    last = value[:, 256:]
    middle = jnp.where((lane >= 32) & (lane < 64), pltpu.roll(last, 96, 1), value[:, 128:256])
    last = jnp.where(lane[:half] < 64, last[:half], pltpu.roll(last[half:], 64, 1))
    out[:rows] = value[:, :128].astype(BF)
    out[rows : 2 * rows] = middle.astype(BF)
    out[2 * rows :] = last.astype(BF)


def resampled(image, offsets, n, table, rows_apart, lanes_apart):
    row_band = band(rows_apart, offsets[n, 0] - 3, table, offsets[n, 2])
    lane_band = band(lanes_apart, LEAD + offsets[n, 1] - 3, table, offsets[n, 3])
    return filtered(image, row_band, lane_band)


def pair_looks(first, partners, looks):
    sums = []
    for _, image, turned, _ in partners:
        sums.append(row_sum(first, image))
        sums.append(row_sum(first, turned))
    maps = looks_of(jnp.concatenate(sums, axis=0), looks)
    count = sums[0].shape[0]
    total = jnp.zeros((count, 128), F32)
    for i, (s, _, _, power) in enumerate(partners):
        for c in range(2):
            one = maps[(2 * i + c) * count : (2 * i + c + 1) * count]
            total = total + pltpu.roll(one, SLOT * (2 + 2 * s + c), 1)
        total = total + pltpu.roll(power, SLOT * (3 + 2 * SPAN + s), 1)
    return total


def resample_kernel(offsets, table, images, z, turned, powers):
    dates, rows, _ = images.shape
    looks = look_matrix()
    rows_apart, lanes_apart = row_distance(rows), lane_distance()
    for n in range(dates):
        value = resampled(images[n], offsets, n, table, rows_apart, lanes_apart)
        z[n] = value.astype(BF)
        turned[n] = crossed(value).astype(BF)
        powers[n] = looks_of(row_sum(z[n], z[n]), looks)


def own_kernel(z, turned, powers, out):
    dates = z.shape[0]
    looks = look_matrix()
    for n in range(dates):
        total = pltpu.roll(powers[n], SLOT * (2 + 2 * SPAN), 1)
        spans = [s for s in range(SPAN) if n + s + 1 < dates]
        if spans:
            partners = [(s, z[n + s + 1], turned[n + s + 1], powers[n + s + 1]) for s in spans]
            total = total + pair_looks(z[n], partners, looks)
        out[n] = total


def later_kernel(offsets, table, later, z, out):
    dates, rows, _ = later.shape
    looks = look_matrix()
    rows_apart, lanes_apart = row_distance(rows), lane_distance()
    found = []
    for n in range(dates):
        value = resampled(later[n], offsets, n, table, rows_apart, lanes_apart)
        image = value.astype(BF)
        power = looks_of(row_sum(image, image), looks)
        found.append((image, crossed(value).astype(BF), power))
    for n in range(dates):
        partners = [(m - n + dates - 1,) + found[m] for m in range(n + 1)]
        out[n] = pair_looks(z[n], partners, looks)


def reference_kernel(ref, part, later_part, z, near, below, above, out):
    dates = part.shape[0]
    rows = z.shape[1]
    looks = look_matrix()
    size, members = lax.axis_size("z"), part.shape[0]
    apart = (lax.axis_index("z") - ref[0] // members) % size
    from_below = (apart >= 2) & (apart <= 4)
    from_above = (apart >= 5) & (apart <= 6)

    def chosen(start, count):
        at = slice(start, start + count)
        value = jnp.where(from_below, below[at].astype(F32), near[at].astype(F32))
        return jnp.where(from_above, above[at].astype(F32), value)

    middle = chosen(rows, rows)
    last = chosen(2 * rows, rows // 2)
    last = jnp.concatenate([last, pltpu.roll(last, 64, 1)], axis=0)
    last = jnp.where(iota((rows, 128), 1) < 64, last, pltpu.roll(middle, 32, 1))
    value = jnp.concatenate([chosen(0, rows), middle, last], axis=1)
    turned = crossed(value).astype(BF)
    value = value.astype(BF)
    for n in range(dates):
        maps = looks_of(jnp.concatenate([row_sum(z[n], value), row_sum(z[n], turned)], axis=0), looks)
        count = maps.shape[0] // 2
        total = part[n] + maps[:count] + pltpu.roll(maps[count:], SLOT, 1)
        if n >= dates - SPAN:
            total = total + later_part[n - dates + SPAN]
        out[n] = total


def finish_kernel(on, got, ref_ifg, pair_ifg, coherence):
    slabs, count, _ = got.shape
    date, dates = lax.axis_index(DATE), lax.axis_size(DATE)
    slab = iota((count, 128), 1) // SLOT

    def gathered(m):
        total = jnp.zeros((count, 128), F32)
        for j in range(slabs):
            moved = pltpu.roll(got[j], SLOT * ((j - m) % slabs), 1)
            total = jnp.where(slab == j, moved, total)
        return total * (1.0 / (LOOK_R * LOOK_C))

    ref_ifg[0, 0] = gathered(0)
    ref_ifg[0, 1] = gathered(1)
    own = jnp.sqrt(gathered(2 + 2 * SPAN) + EPS)
    for s in range(SPAN):
        usable = (on[0, s] == 1) & (date + s + 1 < dates)
        re, im = gathered(2 + 2 * s), gathered(3 + 2 * s)
        other = jnp.sqrt(gathered(3 + 2 * SPAN + s) + EPS)
        coh = jnp.sqrt(re * re + im * im) / (own * other)
        pair_ifg[0, s, 0] = jnp.where(usable, re, 0.0)
        pair_ifg[0, s, 1] = jnp.where(usable, im, 0.0)
        coherence[0, s] = jnp.where(usable, coh, 0.0)


SMEM = pl.BlockSpec(memory_space=pltpu.SMEM)
VMEM = pl.BlockSpec(memory_space=pltpu.VMEM)


def call(kernel, scalars, arrays, outs, flops, scratch=()):
    moved = sum(a.size * a.dtype.itemsize for a in arrays)
    out_shape = [jax.ShapeDtypeStruct(s, d) for s, d in outs]
    single = len(out_shape) == 1
    return pl.pallas_call(
        kernel,
        out_shape=out_shape[0] if single else out_shape,
        in_specs=[SMEM] * len(scalars) + [VMEM] * len(arrays),
        out_specs=VMEM if single else [VMEM] * len(out_shape),
        scratch_shapes=list(scratch),
        compiler_params=pltpu.CompilerParams(vmem_limit_bytes=40 * 2**20),
        cost_estimate=pl.CostEstimate(flops=flops, bytes_accessed=moved, transcendentals=0),
    )(*scalars, *arrays)


def on_device(table, slc, coarse, fraction, pair_on, ref_date):
    _, _, rows, cols = slc.shape
    members = lax.axis_size("y") * lax.axis_size("core")
    halves = lax.axis_size("row")
    slabs = members * halves
    groups = lax.axis_size(FAR)
    all_rows = rows * halves
    count = all_rows // LOOK_R
    ref = ref_date[0]

    anywhere = pl.BlockSpec(memory_space=pl.ANY)
    packed = pl.pallas_call(
        pack_kernel,
        out_shape=jax.ShapeDtypeStruct((slabs, rows, LANES), BF),
        in_specs=[anywhere] * 3,
        out_specs=VMEM,
        scratch_shapes=[
            pltpu.VMEM((2, rows, cols + 256), BF),
            pltpu.SMEM((1, 2), jnp.int32),
            pltpu.SMEM((1, 2), jnp.int32),
            pltpu.SemaphoreType.DMA((2,)),
            pltpu.SemaphoreType.DMA((2,)),
        ],
        compiler_params=pltpu.CompilerParams(vmem_limit_bytes=60 * 2**20),
        cost_estimate=pl.CostEstimate(flops=10**8, bytes_accessed=2 * 10**6, transcendentals=0),
    )(coarse, fraction, slc)
    images = lax.all_to_all(packed, NEAR, 0, 0).reshape(members, all_rows, LANES)

    cand = lax.dynamic_index_in_dim(images, ref % members, 0, keepdims=False)
    cand = call(candidate_kernel, [], [cand], [((all_rows * 5 // 2, 128), BF)], 10**8)
    size = lax.axis_size("z")

    def around(value, by):
        return lax.ppermute(value, "z", [(i, (i + by) % size) for i in range(size)])

    got = lax.ppermute(cand, "xl", [(0, 1), (1, 0)])
    offsets = images[:, :4, SPARE].astype(jnp.int32)
    sums = (members, count, 128)
    z, turned, powers = call(
        resample_kernel, [offsets, table], [images],
        [(images.shape, BF), (images.shape, BF), (sums, F32)], 4 * 10**9,
    )
    got, z = lax.optimization_barrier((got, z))
    q = jnp.where(lax.axis_index("xl") == ref // (members * size), cand, got)
    apart = (lax.axis_index("z") - ref // members) % size
    below, above = around(q, 1), around(q, -1)
    part = call(own_kernel, [], [z, turned, powers], [(sums, F32)], 2 * 10**9)
    below, part = lax.optimization_barrier((below, part))
    q = jnp.where(apart == 1, below, jnp.where(apart == size - 1, above, q))
    below, above = around(q, 3), around(q, -3)

    later = lax.ppermute(images[:SPAN], FAR, [(i + 1, i) for i in range(groups - 1)])

    later_offsets = later[:, :4, SPARE].astype(jnp.int32)
    later_part = call(
        later_kernel, [later_offsets, table], [later, z[members - SPAN :]],
        [((SPAN, count, 128), F32)], 2 * 10**9,
    )
    maps = call(
        reference_kernel, [ref_date], [part, later_part, z, q, below, above], [(sums, F32)], 10**9
    )
    got = lax.all_to_all(maps.reshape(slabs, count // halves, 128), NEAR, 0, 0)
    small = (count // halves, 128)
    return call(
        finish_kernel, [pair_on], [got],
        [((1, 2) + small, F32), ((1, SPAN, 2) + small, F32), ((1, SPAN) + small, F32)], 10**7,
    )


def solution(mesh):
    shape = GRID + (mesh.shape["row"],)
    grid = Mesh(mesh.devices.reshape(shape), DATE + ("row",))
    table = tap_table()

    def program(slc, coarse, fraction, pair_on, ref_date):
        return tuple(
            jax.shard_map(
                on_device,
                mesh=grid,
                in_specs=(
                    P(),
                    P(DATE, None, "row", None),
                    P(DATE, None),
                    P(DATE, None),
                    P(DATE, None),
                    P(),
                ),
                out_specs=(
                    P(DATE, None, "row", None),
                    P(DATE, None, None, "row", None),
                    P(DATE, None, "row", None),
                ),
                check_vma=False,
            )(jnp.asarray(table), slc, coarse, fraction, pair_on, ref_date)
        )

    return program
```

```python
import jax
import jax.numpy as jnp
import ml_dtypes
import numpy as np
from jax import lax
from jax.experimental import pallas as pl
from jax.experimental.pallas import tpu as pltpu
from jax.sharding import Mesh, PartitionSpec as P

NFRAC = 64
SPAN = 3
LOOK_R = 5
LOOK_C = 20
EPS = 1e-06
BF = jnp.bfloat16
F32 = jnp.float32

GRID = (2, 8, 4, 2)
DATE = ("xl", "z", "y", "core")
NEAR = ("xl", "y", "core")
RUNS = 2
HALO = 16

SLAB = 160
WIN = 192
LEAD = 16
LANES = 2 * WIN
SPARE = 190
SLOT = SLAB // LOOK_C


def tap_table():
    x = np.arange(8)[None, :] - 3.0 - np.arange(NFRAC)[:, None] / NFRAC
    w = np.sinc(x) * (0.54 + 0.46 * np.cos(np.pi * x / 4.0))
    taps = (w / w.sum(axis=1, keepdims=True)).astype(np.float32)
    return taps.astype(ml_dtypes.bfloat16).astype(np.float32)


def iota(shape, dim):
    return lax.broadcasted_iota(jnp.int32, shape, dim)


def dot(a, b):
    return jnp.dot(a, b, preferred_element_type=F32)


def row_order(rows, columns):
    looks = rows // LOOK_R
    out = iota((rows, columns), 0)
    return (out % looks) * LOOK_R + out // looks


def row_distance(rows):
    source = iota((rows, rows + HALO), 1)
    first = lax.axis_index("row") == 0
    source = jnp.where((source < rows) | first, source, source - rows - HALO)
    return source - row_order(rows, rows + HALO)


def placed(distance, shift, table, index):
    total = jnp.zeros(distance.shape, F32)
    for k in range(8):
        total = jnp.where(distance == shift + k, table[index, k], total)
    return total


def lane_band_of(shift, table, index):
    lane = iota((8, 128), 1)
    base = placed(jnp.where(lane == 0, 0, 128 - lane), shift, table, index)
    turned = pltpu.roll(jnp.broadcast_to(base[:1], (128, 128)), 0, 1, stride=1, stride_axis=0)
    upper = iota((128, 128), 1) <= iota((128, 128), 0)
    return jnp.concatenate(
        [jnp.where(upper, turned, 0.0), jnp.where(upper, 0.0, turned)], axis=0
    ).astype(BF)


def filtered(image, row_band, lane_band):
    rows = row_band.shape[0]
    fit = dot(row_band, image).astype(BF)
    last = jnp.concatenate([fit[:, 256:], jnp.zeros((rows, 128), BF)], axis=1)
    found = dot(jnp.concatenate([fit[:, :256], fit[:, 128:], last], axis=0), lane_band)
    return jnp.concatenate([found[:rows], found[rows : 2 * rows], found[2 * rows :]], axis=1)


def crossed(value):
    turned = pltpu.roll(value, WIN, 1)
    return jnp.where(iota(value.shape, 1) < WIN, -turned, turned)


def look_matrix():
    lane = iota((LANES, 128), 0)
    col = jnp.where(lane < WIN, lane, lane - WIN)
    distance = col - LOOK_C * iota((LANES, 128), 1)
    inside = (col < SLAB) & (distance >= 0) & (distance < LOOK_C)
    return jnp.where(inside, 1.0, 0.0).astype(BF)


def looks_of(sums, looks):
    high = sums.astype(BF)
    low = (sums - high.astype(F32)).astype(BF)
    return dot(high, looks) + dot(low, looks)


def row_sum(first, second):
    rows = first.shape[0] // LOOK_R
    total = None
    for j in range(LOOK_R):
        part = first[j * rows : (j + 1) * rows].astype(F32) * second[j * rows : (j + 1) * rows].astype(F32)
        total = part if total is None else total + part
    return total


def pack_kernel(coarse, fraction, x, out, wide, shifts, taps, image_sem, small_sem):
    _, _, rows, cols = x.shape
    copies = [
        pltpu.make_async_copy(x.at[0, p], wide.at[p, :, pl.ds(128, cols)], image_sem.at[p])
        for p in range(2)
    ]
    copies.append(pltpu.make_async_copy(coarse, shifts, small_sem.at[0]))
    copies.append(pltpu.make_async_copy(fraction, taps, small_sem.at[1]))
    for copy in copies:
        copy.start()
    for p in range(2):
        wide[p, :, :128] = jnp.zeros((rows, 128), BF)
        wide[p, :, 128 + cols :] = jnp.zeros((rows, 128), BF)
    lane = iota((rows, LANES), 1)
    row = iota((rows, LANES), 0)
    for copy in copies:
        copy.wait()
    own = jnp.where(row == 0, shifts[0, 0], jnp.where(row == 1, shifts[0, 1], 0))
    own = jnp.where(row == 2, taps[0, 0], jnp.where(row == 3, taps[0, 1], own))
    own = own.astype(F32)
    for j in range(out.shape[0]):
        start = 128 + SLAB * j - LEAD
        base, off = start // 128 * 128, start % 128
        first = pltpu.roll(wide[0, :, base : base + LANES].astype(F32), (LANES - off) % LANES, 1)
        second = pltpu.roll(wide[1, :, base : base + LANES].astype(F32), WIN - off, 1)
        value = jnp.where(lane < WIN, first, second)
        out[j] = jnp.where(lane == SPARE, own, value).astype(BF)


def candidate_kernel(image, out):
    rows = image.shape[0]
    order = jnp.where(row_order(rows, rows) == iota((rows, rows), 1), 1.0, 0.0).astype(BF)
    shift = jnp.where(iota((256, 128), 0) - iota((256, 128), 1) == LEAD, 1.0, 0.0).astype(BF)
    value = filtered(image[...], order, shift).astype(BF)
    for t in range(LANES // 128):
        out[t * rows : (t + 1) * rows] = value[:, t * 128 : (t + 1) * 128]


def resampled(image, edge, offsets, n, table, rows_apart):
    row_band = placed(rows_apart, offsets[n, 0] - 3, table, offsets[n, 2]).astype(BF)
    lane_band = lane_band_of(LEAD + offsets[n, 1] - 3, table, offsets[n, 3])
    return filtered(jnp.concatenate([image, edge], axis=0), row_band, lane_band)


def add_pairs(out, start, pairs, looks):
    sums = []
    for _, _, first, second, turned, _ in pairs:
        sums.append(row_sum(first, second))
        sums.append(row_sum(first, turned))
    count = sums[0].shape[0]
    maps = looks_of(jnp.concatenate(sums, axis=0), looks)
    totals = dict(start)
    for i, (n, s, _, _, _, power) in enumerate(pairs):
        for c in range(2):
            one = maps[(2 * i + c) * count : (2 * i + c + 1) * count]
            one = pltpu.roll(one, SLOT * (2 + 2 * s + c), 1)
            totals[n] = totals[n] + one if n in totals else one
        totals[n] = totals[n] + pltpu.roll(power, SLOT * (3 + 2 * SPAN + s), 1)
    for n, total in totals.items():
        out[n] = total


def resample_kernel(offsets, table, images, edges, z, turned, powers):
    dates, rows, _ = images.shape
    rows_apart = row_distance(rows)
    sums = []
    for n in range(dates):
        value = resampled(images[n], edges[n], offsets, n, table, rows_apart)
        z[n] = value.astype(BF)
        turned[n] = crossed(value).astype(BF)
        sums.append(row_sum(z[n], z[n]))
    powers[...] = looks_of(jnp.concatenate(sums, axis=0), look_matrix()).reshape(powers.shape)


def own_kernel(z, turned, powers, out):
    dates = z.shape[0] // RUNS
    looks = look_matrix()
    for run in range(0, z.shape[0], dates):
        start = {n: pltpu.roll(powers[n], SLOT * (2 + 2 * SPAN), 1) for n in range(run, run + dates)}
        pairs = [
            (n, s, z[n], z[n + s + 1], turned[n + s + 1], powers[n + s + 1])
            for n in range(run, run + dates)
            for s in range(SPAN)
            if n + s + 1 < run + dates
        ]
        add_pairs(out, start, pairs, looks)


def later_kernel(offsets, table, later, edges, z, out):
    rows = later.shape[1]
    members = z.shape[0] // RUNS
    looks = look_matrix()
    rows_apart = row_distance(rows)
    last = lax.axis_index("z") == lax.axis_size("z") - 1
    found, sums = [], []
    for run in range(RUNS):
        base = jnp.where(last, SPAN * (RUNS - 1), SPAN * run)
        for n in range(SPAN):
            value = resampled(later[base + n], edges[base + n], offsets, base + n, table, rows_apart)
            image = value.astype(BF)
            sums.append(row_sum(image, image))
            found.append((image, crossed(value).astype(BF)))
    powers = looks_of(jnp.concatenate(sums, axis=0), looks)
    count = sums[0].shape[0]
    pairs = []
    for run in range(RUNS):
        for n in range(SPAN):
            first = z[(run + 1) * members - SPAN + n]
            for m in range(n + 1):
                at = run * SPAN + m
                power = powers[at * count : (at + 1) * count]
                pairs.append((run * SPAN + n, m - n + SPAN - 1, first) + found[at] + (power,))
    add_pairs(out, {}, pairs, looks)


def reference_kernel(ref, part, later_part, z, near, below, above, out):
    dates = part.shape[0]
    rows = z.shape[1]
    size, members = lax.axis_size("z"), dates // RUNS
    apart = (lax.axis_index("z") - ref[0] // members) % size
    from_below = (apart >= 2) & (apart <= 4)
    from_above = (apart >= 5) & (apart <= 6)
    tiles = []
    for t in range(LANES // 128):
        at = slice(t * rows, (t + 1) * rows)
        value = jnp.where(from_below, below[at].astype(F32), near[at].astype(F32))
        tiles.append(jnp.where(from_above, above[at].astype(F32), value))
    value = jnp.concatenate(tiles, axis=1)
    turned = crossed(value).astype(BF)
    value = value.astype(BF)
    sums = []
    for n in range(dates):
        sums.append(row_sum(z[n], value))
        sums.append(row_sum(z[n], turned))
    maps = looks_of(jnp.concatenate(sums, axis=0), look_matrix())
    count = sums[0].shape[0]
    for n in range(dates):
        at = 2 * n * count
        total = part[n] + maps[at : at + count] + pltpu.roll(maps[at + count : at + 2 * count], SLOT, 1)
        if n % members >= members - SPAN:
            total = total + later_part[n // members * SPAN + n % members - members + SPAN]
        out[n] = total


def finish_kernel(on, got, ref_ifg, pair_ifg, coherence):
    slabs, count, _ = got.shape
    date, dates = lax.axis_index(DATE), lax.axis_size(DATE)
    slab = iota((count, 128), 1) // SLOT

    def gathered(m):
        total = jnp.zeros((count, 128), F32)
        for j in range(slabs):
            moved = pltpu.roll(got[j], SLOT * ((j - m) % slabs), 1)
            total = jnp.where(slab == j, moved, total)
        return total * (1.0 / (LOOK_R * LOOK_C))

    ref_ifg[0, 0] = gathered(0)
    ref_ifg[0, 1] = gathered(1)
    own = jnp.sqrt(gathered(2 + 2 * SPAN) + EPS)
    for s in range(SPAN):
        usable = (on[0, s] == 1) & (date + s + 1 < dates)
        re, im = gathered(2 + 2 * s), gathered(3 + 2 * s)
        other = jnp.sqrt(gathered(3 + 2 * SPAN + s) + EPS)
        coh = jnp.sqrt(re * re + im * im) / (own * other)
        pair_ifg[0, s, 0] = jnp.where(usable, re, 0.0)
        pair_ifg[0, s, 1] = jnp.where(usable, im, 0.0)
        coherence[0, s] = jnp.where(usable, coh, 0.0)


SMEM = pl.BlockSpec(memory_space=pltpu.SMEM)
VMEM = pl.BlockSpec(memory_space=pltpu.VMEM)


def call(kernel, scalars, arrays, outs, flops, scratch=()):
    moved = sum(a.size * a.dtype.itemsize for a in arrays)
    out_shape = [jax.ShapeDtypeStruct(s, d) for s, d in outs]
    single = len(out_shape) == 1
    return pl.pallas_call(
        kernel,
        out_shape=out_shape[0] if single else out_shape,
        in_specs=[SMEM] * len(scalars) + [VMEM] * len(arrays),
        out_specs=VMEM if single else [VMEM] * len(out_shape),
        scratch_shapes=list(scratch),
        compiler_params=pltpu.CompilerParams(vmem_limit_bytes=40 * 2**20),
        cost_estimate=pl.CostEstimate(flops=flops, bytes_accessed=moved, transcendentals=0),
    )(*scalars, *arrays)


def on_device(table, slc, coarse, fraction, pair_on, ref_date):
    _, _, rows, cols = slc.shape
    slabs = lax.axis_size(NEAR)
    members = slabs // RUNS
    size = lax.axis_size("z")
    count = rows // LOOK_R
    row = lax.axis_index("row")
    ref = ref_date[0]

    anywhere = pl.BlockSpec(memory_space=pl.ANY)
    packed = pl.pallas_call(
        pack_kernel,
        out_shape=jax.ShapeDtypeStruct((slabs, rows, LANES), BF),
        in_specs=[anywhere] * 3,
        out_specs=VMEM,
        scratch_shapes=[
            pltpu.VMEM((2, rows, cols + 256), BF),
            pltpu.SMEM((1, 2), jnp.int32),
            pltpu.SMEM((1, 2), jnp.int32),
            pltpu.SemaphoreType.DMA((2,)),
            pltpu.SemaphoreType.DMA((2,)),
        ],
        compiler_params=pltpu.CompilerParams(vmem_limit_bytes=60 * 2**20),
        cost_estimate=pl.CostEstimate(flops=10**8, bytes_accessed=2 * 10**6, transcendentals=0),
    )(coarse, fraction, slc)
    images = lax.all_to_all(packed, NEAR, 0, 0)

    edge = jnp.where(row == 0, images[:, rows - HALO :], images[:, :HALO])
    edges = lax.ppermute(edge, "row", [(0, 1), (1, 0)])

    def first_dates(value):
        return jnp.concatenate([value[n : n + SPAN] for n in range(0, slabs, members)], axis=0)

    later = lax.ppermute(first_dates(images), "z", [((i + 1) % size, i) for i in range(size)])
    later_edges = lax.ppermute(
        first_dates(edge), ("z", "row"),
        [((i + 1) % size * 2 + 1 - r, i * 2 + r) for i in range(size) for r in range(2)],
    )

    cand = lax.dynamic_index_in_dim(
        images, ref // (members * size) * members + ref % members, 0, keepdims=False
    )
    q = call(candidate_kernel, [], [cand], [((LANES // 128 * rows, 128), BF)], 10**8)

    def around(value, by):
        return lax.ppermute(value, "z", [(i, (i + by) % size) for i in range(size)])

    apart = (lax.axis_index("z") - ref // members) % size
    below, above = around(q, 1), around(q, -1)
    near = jnp.where(apart == 1, below, jnp.where(apart == size - 1, above, q))
    below, above = around(near, 3), around(near, -3)

    sums = (slabs, count, 128)
    offsets = images[:, :4, SPARE].astype(jnp.int32)
    z, turned, powers = call(
        resample_kernel, [offsets, table], [images, edges],
        [(images.shape, BF), (images.shape, BF), (sums, F32)], 4 * 10**9,
    )
    part = call(own_kernel, [], [z, turned, powers], [(sums, F32)], 2 * 10**9)
    later_offsets = later[:, :4, SPARE].astype(jnp.int32)
    later_part = call(
        later_kernel, [later_offsets, table], [later, later_edges, z],
        [((RUNS * SPAN, count, 128), F32)], 2 * 10**9,
    )
    maps = call(
        reference_kernel, [ref_date], [part, later_part, z, near, below, above],
        [(sums, F32)], 10**9,
    )
    got = lax.all_to_all(maps, NEAR, 0, 0)
    small = (count, 128)
    return call(
        finish_kernel, [pair_on], [got],
        [((1, 2) + small, F32), ((1, SPAN, 2) + small, F32), ((1, SPAN) + small, F32)], 10**7,
    )


def solution(mesh):
    shape = GRID + (mesh.shape["row"],)
    grid = Mesh(mesh.devices.reshape(shape), DATE + ("row",))
    table = tap_table()

    def program(slc, coarse, fraction, pair_on, ref_date):
        return tuple(
            jax.shard_map(
                on_device,
                mesh=grid,
                in_specs=(
                    P(),
                    P(DATE, None, "row", None),
                    P(DATE, None),
                    P(DATE, None),
                    P(DATE, None),
                    P(),
                ),
                out_specs=(
                    P(DATE, None, "row", None),
                    P(DATE, None, None, "row", None),
                    P(DATE, None, "row", None),
                ),
                check_vma=False,
            )(jnp.asarray(table), slc, coarse, fraction, pair_on, ref_date)
        )

    return program
```

```python
import jax
import jax.numpy as jnp
import ml_dtypes
import numpy as np
from jax import lax
from jax.experimental import pallas as pl
from jax.experimental.pallas import tpu as pltpu
from jax.sharding import Mesh, PartitionSpec as P

NFRAC = 64
SPAN = 3
LOOK_R = 5
LOOK_C = 20
EPS = 1e-06
BF = jnp.bfloat16
F32 = jnp.float32

GRID = (2, 8, 4, 2)
DATE = ("xl", "z", "y", "core")
NEAR = ("xl", "y", "core")
RUNS = 2
HALO = 16

SLAB = 160
WIN = 192
LEAD = 16
LANES = 2 * WIN
SPARE = 190
SLOT = SLAB // LOOK_C


def tap_table():
    x = np.arange(8)[None, :] - 3.0 - np.arange(NFRAC)[:, None] / NFRAC
    w = np.sinc(x) * (0.54 + 0.46 * np.cos(np.pi * x / 4.0))
    taps = (w / w.sum(axis=1, keepdims=True)).astype(np.float32)
    return taps.astype(ml_dtypes.bfloat16).astype(np.float32)


def iota(shape, dim):
    return lax.broadcasted_iota(jnp.int32, shape, dim)


def dot(a, b):
    return jnp.dot(a, b, preferred_element_type=F32)


def row_order(rows, columns):
    looks = rows // LOOK_R
    out = iota((rows, columns), 0)
    return (out % looks) * LOOK_R + out // looks


def row_distance(rows):
    source = iota((rows, rows + HALO), 1)
    first = lax.axis_index("row") == 0
    source = jnp.where((source < rows) | first, source, source - rows - HALO)
    return source - row_order(rows, rows + HALO)


def placed(distance, shift, table, index):
    total = jnp.zeros(distance.shape, F32)
    for k in range(8):
        total = jnp.where(distance == shift + k, table[index, k], total)
    return total


def lane_band_of(shift, table, index):
    lane = iota((8, 128), 1)
    base = placed(jnp.where(lane == 0, 0, 128 - lane), shift, table, index)
    turned = pltpu.roll(jnp.broadcast_to(base[:1], (128, 128)), 0, 1, stride=1, stride_axis=0)
    upper = iota((128, 128), 1) <= iota((128, 128), 0)
    return jnp.concatenate(
        [jnp.where(upper, turned, 0.0), jnp.where(upper, 0.0, turned)], axis=0
    ).astype(BF)


def filtered(image, row_band, lane_band):
    rows = row_band.shape[0]
    fit = dot(row_band, image).astype(BF)
    last = jnp.concatenate([fit[:, 256:], jnp.zeros((rows, 128), BF)], axis=1)
    found = dot(jnp.concatenate([fit[:, :256], fit[:, 128:], last], axis=0), lane_band)
    return jnp.concatenate([found[:rows], found[rows : 2 * rows], found[2 * rows :]], axis=1)


def crossed(value):
    turned = pltpu.roll(value, WIN, 1)
    return jnp.where(iota(value.shape, 1) < WIN, -turned, turned)


def look_matrix():
    lane = iota((LANES, 128), 0)
    col = jnp.where(lane < WIN, lane, lane - WIN)
    distance = col - LOOK_C * iota((LANES, 128), 1)
    inside = (col < SLAB) & (distance >= 0) & (distance < LOOK_C)
    return jnp.where(inside, 1.0, 0.0).astype(BF)


def looks_of(sums, looks):
    high = sums.astype(BF)
    low = (sums - high.astype(F32)).astype(BF)
    return dot(high, looks) + dot(low, looks)


def row_sum(first, second):
    rows = first.shape[0] // LOOK_R
    total = None
    for j in range(LOOK_R):
        part = first[j * rows : (j + 1) * rows].astype(F32) * second[j * rows : (j + 1) * rows].astype(F32)
        total = part if total is None else total + part
    return total


def pack_kernel(coarse, fraction, x, out, wide, packed, shifts, taps, in_sem, out_sem, small_sem):
    _, _, rows, cols = x.shape
    pieces = in_sem.shape[0] // 2
    width = cols // pieces
    small = [
        pltpu.make_async_copy(coarse, shifts, small_sem.at[0]),
        pltpu.make_async_copy(fraction, taps, small_sem.at[1]),
    ]
    incoming = [
        pltpu.make_async_copy(
            x.at[0, p, :, pl.ds(c * width, width)],
            wide.at[p, :, pl.ds(128 + c * width, width)],
            in_sem.at[2 * c + p],
        )
        for c in range(pieces)
        for p in range(2)
    ]
    for copy in small + incoming:
        copy.start()
    for p in range(2):
        wide[p, :, :128] = jnp.zeros((rows, 128), BF)
        wide[p, :, 128 + cols :] = jnp.zeros((rows, 128), BF)
    lane = iota((rows, LANES), 1)
    row = iota((rows, LANES), 0)
    for copy in small:
        copy.wait()
    own = jnp.where(row == 0, shifts[0, 0], jnp.where(row == 1, shifts[0, 1], 0))
    own = jnp.where(row == 2, taps[0, 0], jnp.where(row == 3, taps[0, 1], own))
    own = own.astype(F32)
    here = 0
    outgoing = []
    for j in range(out.shape[0]):
        start = 128 + SLAB * j - LEAD
        base, off = start // 128 * 128, start % 128
        while here < pieces and 128 + here * width < base + LANES:
            incoming[2 * here].wait()
            incoming[2 * here + 1].wait()
            here += 1
        first = pltpu.roll(wide[0, :, base : base + LANES].astype(F32), (LANES - off) % LANES, 1)
        second = pltpu.roll(wide[1, :, base : base + LANES].astype(F32), WIN - off, 1)
        value = jnp.where(lane < WIN, first, second)
        packed[j] = jnp.where(lane == SPARE, own, value).astype(BF)
        outgoing.append(pltpu.make_async_copy(packed.at[j], out.at[j], out_sem.at[j]))
        outgoing[-1].start()
    for copy in outgoing:
        copy.wait()


def candidate_kernel(image, out):
    rows = image.shape[0]
    order = jnp.where(row_order(rows, rows) == iota((rows, rows), 1), 1.0, 0.0).astype(BF)
    shift = jnp.where(iota((256, 128), 0) - iota((256, 128), 1) == LEAD, 1.0, 0.0).astype(BF)
    value = filtered(image[...], order, shift).astype(BF)
    for t in range(LANES // 128):
        out[t * rows : (t + 1) * rows] = value[:, t * 128 : (t + 1) * 128]


def resampled(image, offsets, n, table, rows_apart):
    row_band = placed(rows_apart, offsets[n, 0] - 3, table, offsets[n, 2]).astype(BF)
    lane_band = lane_band_of(LEAD + offsets[n, 1] - 3, table, offsets[n, 3])
    return filtered(image, row_band, lane_band)


def add_pairs(out, start, pairs, looks):
    sums = []
    for _, _, first, second, turned, _ in pairs:
        sums.append(row_sum(first, second))
        sums.append(row_sum(first, turned))
    count = sums[0].shape[0]
    maps = looks_of(jnp.concatenate(sums, axis=0), looks)
    totals = dict(start)
    for i, (n, s, _, _, _, power) in enumerate(pairs):
        for c in range(2):
            one = maps[(2 * i + c) * count : (2 * i + c + 1) * count]
            one = pltpu.roll(one, SLOT * (2 + 2 * s + c), 1)
            totals[n] = totals[n] + one if n in totals else one
        totals[n] = totals[n] + pltpu.roll(power, SLOT * (3 + 2 * SPAN + s), 1)
    for n, total in totals.items():
        out[n] = total


def resample_kernel(offsets, table, images, edges, z, turned, powers):
    dates, rows, _ = images.shape
    rows_apart = row_distance(rows)
    sums = []
    for n in range(dates):
        image = jnp.concatenate([images[n], edges[n]], axis=0)
        value = resampled(image, offsets, n, table, rows_apart)
        z[n] = value.astype(BF)
        turned[n] = crossed(value).astype(BF)
        sums.append(row_sum(z[n], z[n]))
    powers[...] = looks_of(jnp.concatenate(sums, axis=0), look_matrix()).reshape(powers.shape)


def own_kernel(z, turned, powers, out):
    dates = z.shape[0] // RUNS
    looks = look_matrix()
    for run in range(0, z.shape[0], dates):
        start = {n: pltpu.roll(powers[n], SLOT * (2 + 2 * SPAN), 1) for n in range(run, run + dates)}
        pairs = [
            (n, s, z[n], z[n + s + 1], turned[n + s + 1], powers[n + s + 1])
            for n in range(run, run + dates)
            for s in range(SPAN)
            if n + s + 1 < run + dates
        ]
        add_pairs(out, start, pairs, looks)


def later_kernel(offsets, table, later, z, out):
    rows = z.shape[1]
    members = z.shape[0] // RUNS
    looks = look_matrix()
    rows_apart = row_distance(rows)
    last = lax.axis_index("z") == lax.axis_size("z") - 1
    found, sums = [], []
    for run in range(RUNS):
        base = jnp.where(last, SPAN * (RUNS - 1), SPAN * run)
        for n in range(SPAN):
            value = resampled(later[base + n], offsets, base + n, table, rows_apart)
            image = value.astype(BF)
            sums.append(row_sum(image, image))
            found.append((image, crossed(value).astype(BF)))
    powers = looks_of(jnp.concatenate(sums, axis=0), looks)
    count = sums[0].shape[0]
    pairs = []
    for run in range(RUNS):
        for n in range(SPAN):
            first = z[(run + 1) * members - SPAN + n]
            for m in range(n + 1):
                at = run * SPAN + m
                power = powers[at * count : (at + 1) * count]
                pairs.append((run * SPAN + n, m - n + SPAN - 1, first) + found[at] + (power,))
    add_pairs(out, {}, pairs, looks)


def reference_kernel(ref, part, later_part, z, near, below, above, out):
    dates = part.shape[0]
    rows = z.shape[1]
    size, members = lax.axis_size("z"), dates // RUNS
    apart = (lax.axis_index("z") - ref[0] // members) % size
    from_below = (apart >= 2) & (apart <= 4)
    from_above = (apart >= 5) & (apart <= 6)
    tiles = []
    for t in range(LANES // 128):
        at = slice(t * rows, (t + 1) * rows)
        value = jnp.where(from_below, below[at].astype(F32), near[at].astype(F32))
        tiles.append(jnp.where(from_above, above[at].astype(F32), value))
    value = jnp.concatenate(tiles, axis=1)
    turned = crossed(value).astype(BF)
    value = value.astype(BF)
    sums = []
    for n in range(dates):
        sums.append(row_sum(z[n], value))
        sums.append(row_sum(z[n], turned))
    maps = looks_of(jnp.concatenate(sums, axis=0), look_matrix())
    count = sums[0].shape[0]
    for n in range(dates):
        at = 2 * n * count
        total = part[n] + maps[at : at + count] + pltpu.roll(maps[at + count : at + 2 * count], SLOT, 1)
        if n % members >= members - SPAN:
            total = total + later_part[n // members * SPAN + n % members - members + SPAN]
        out[n] = total


def finish_kernel(on, got, ref_ifg, pair_ifg, coherence):
    slabs, count, _ = got.shape
    date, dates = lax.axis_index(DATE), lax.axis_size(DATE)
    slab = iota((count, 128), 1) // SLOT

    def gathered(m):
        total = jnp.zeros((count, 128), F32)
        for j in range(slabs):
            moved = pltpu.roll(got[j], SLOT * ((j - m) % slabs), 1)
            total = jnp.where(slab == j, moved, total)
        return total * (1.0 / (LOOK_R * LOOK_C))

    ref_ifg[0, 0] = gathered(0)
    ref_ifg[0, 1] = gathered(1)
    own = jnp.sqrt(gathered(2 + 2 * SPAN) + EPS)
    for s in range(SPAN):
        usable = (on[0, s] == 1) & (date + s + 1 < dates)
        re, im = gathered(2 + 2 * s), gathered(3 + 2 * s)
        other = jnp.sqrt(gathered(3 + 2 * SPAN + s) + EPS)
        coh = jnp.sqrt(re * re + im * im) / (own * other)
        pair_ifg[0, s, 0] = jnp.where(usable, re, 0.0)
        pair_ifg[0, s, 1] = jnp.where(usable, im, 0.0)
        coherence[0, s] = jnp.where(usable, coh, 0.0)


SMEM = pl.BlockSpec(memory_space=pltpu.SMEM)
VMEM = pl.BlockSpec(memory_space=pltpu.VMEM)


def call(kernel, scalars, arrays, outs, flops, scratch=()):
    moved = sum(a.size * a.dtype.itemsize for a in arrays)
    out_shape = [jax.ShapeDtypeStruct(s, d) for s, d in outs]
    single = len(out_shape) == 1
    return pl.pallas_call(
        kernel,
        out_shape=out_shape[0] if single else out_shape,
        in_specs=[SMEM] * len(scalars) + [VMEM] * len(arrays),
        out_specs=VMEM if single else [VMEM] * len(out_shape),
        scratch_shapes=list(scratch),
        compiler_params=pltpu.CompilerParams(vmem_limit_bytes=40 * 2**20),
        cost_estimate=pl.CostEstimate(flops=flops, bytes_accessed=moved, transcendentals=0),
    )(*scalars, *arrays)


def on_device(table, slc, coarse, fraction, pair_on, ref_date):
    _, _, rows, cols = slc.shape
    slabs = lax.axis_size(NEAR)
    members = slabs // RUNS
    size = lax.axis_size("z")
    count = rows // LOOK_R
    row = lax.axis_index("row")
    ref = ref_date[0]

    anywhere = pl.BlockSpec(memory_space=pl.ANY)
    packed = pl.pallas_call(
        pack_kernel,
        out_shape=jax.ShapeDtypeStruct((slabs, rows, LANES), BF),
        in_specs=[anywhere] * 3,
        out_specs=anywhere,
        scratch_shapes=[
            pltpu.VMEM((2, rows, cols + 256), BF),
            pltpu.VMEM((slabs, rows, LANES), BF),
            pltpu.SMEM((1, 2), jnp.int32),
            pltpu.SMEM((1, 2), jnp.int32),
            pltpu.SemaphoreType.DMA((8,)),
            pltpu.SemaphoreType.DMA((slabs,)),
            pltpu.SemaphoreType.DMA((2,)),
        ],
        compiler_params=pltpu.CompilerParams(vmem_limit_bytes=60 * 2**20),
        cost_estimate=pl.CostEstimate(flops=10**8, bytes_accessed=2 * 10**6, transcendentals=0),
    )(coarse, fraction, slc)
    images = lax.all_to_all(packed, NEAR, 0, 0)

    edge = jnp.where(row == 0, images[:, rows - HALO :], images[:, :HALO])
    edges = lax.ppermute(edge, "row", [(0, 1), (1, 0)])

    def first_dates(value):
        return jnp.concatenate([value[n : n + SPAN] for n in range(0, slabs, members)], axis=0)

    later = lax.ppermute(
        jnp.concatenate([first_dates(images), first_dates(edges)], axis=1),
        "z", [((i + 1) % size, i) for i in range(size)],
    )

    cand = lax.dynamic_index_in_dim(
        images, ref // (members * size) * members + ref % members, 0, keepdims=False
    )
    q = call(candidate_kernel, [], [cand], [((LANES // 128 * rows, 128), BF)], 10**8)

    def around(value, by):
        return lax.ppermute(value, "z", [(i, (i + by) % size) for i in range(size)])

    apart = (lax.axis_index("z") - ref // members) % size
    below, above = around(q, 1), around(q, -1)

    sums = (slabs, count, 128)
    offsets = images[:, :4, SPARE].astype(jnp.int32)
    z, turned, powers = call(
        resample_kernel, [offsets, table], [images, edges],
        [(images.shape, BF), (images.shape, BF), (sums, F32)], 4 * 10**9,
    )
    below, z = lax.optimization_barrier((below, z))
    near = jnp.where(apart == 1, below, jnp.where(apart == size - 1, above, q))
    below, above = around(near, 3), around(near, -3)
    part = call(own_kernel, [], [z, turned, powers], [(sums, F32)], 2 * 10**9)
    later_offsets = later[:, :4, SPARE].astype(jnp.int32)
    later_part = call(
        later_kernel, [later_offsets, table], [later, z],
        [((RUNS * SPAN, count, 128), F32)], 2 * 10**9,
    )
    maps = call(
        reference_kernel, [ref_date], [part, later_part, z, near, below, above],
        [(sums, F32)], 10**9,
    )
    got = lax.all_to_all(maps, NEAR, 0, 0)
    small = (count, 128)
    return call(
        finish_kernel, [pair_on], [got],
        [((1, 2) + small, F32), ((1, SPAN, 2) + small, F32), ((1, SPAN) + small, F32)], 10**7,
    )


def solution(mesh):
    shape = GRID + (mesh.shape["row"],)
    grid = Mesh(mesh.devices.reshape(shape), DATE + ("row",))
    table = tap_table()

    def program(slc, coarse, fraction, pair_on, ref_date):
        return tuple(
            jax.shard_map(
                on_device,
                mesh=grid,
                in_specs=(
                    P(),
                    P(DATE, None, "row", None),
                    P(DATE, None),
                    P(DATE, None),
                    P(DATE, None),
                    P(),
                ),
                out_specs=(
                    P(DATE, None, "row", None),
                    P(DATE, None, None, "row", None),
                    P(DATE, None, "row", None),
                ),
                check_vma=False,
            )(jnp.asarray(table), slc, coarse, fraction, pair_on, ref_date)
        )

    return program
```

```python
import jax
import jax.numpy as jnp
import ml_dtypes
import numpy as np
from jax import lax
from jax.experimental import pallas as pl
from jax.experimental.pallas import tpu as pltpu
from jax.sharding import Mesh, PartitionSpec as P

NFRAC = 64
SPAN = 3
LOOK_R = 5
LOOK_C = 20
EPS = 1e-06
BF = jnp.bfloat16
F32 = jnp.float32

GRID = (2, 8, 4, 2)
DATE = ("xl", "z", "y", "core")
NEAR = ("xl", "y", "core")
RUNS = 2
HALO = 16

SLAB = 160
WIN = 192
LEAD = 16
LANES = 2 * WIN
SPARE = 190
SLOT = SLAB // LOOK_C


def tap_table():
    x = np.arange(8)[None, :] - 3.0 - np.arange(NFRAC)[:, None] / NFRAC
    w = np.sinc(x) * (0.54 + 0.46 * np.cos(np.pi * x / 4.0))
    taps = (w / w.sum(axis=1, keepdims=True)).astype(np.float32)
    return taps.astype(ml_dtypes.bfloat16).astype(np.float32)


def iota(shape, dim):
    return lax.broadcasted_iota(jnp.int32, shape, dim)


def dot(a, b):
    return jnp.dot(a, b, preferred_element_type=F32)


def row_order(rows, columns):
    looks = rows // LOOK_R
    out = iota((rows, columns), 0)
    return (out % looks) * LOOK_R + out // looks


def row_distance(rows):
    source = iota((rows, rows + HALO), 1)
    first = lax.axis_index("row") == 0
    source = jnp.where((source < rows) | first, source, source - rows - HALO)
    return source - row_order(rows, rows + HALO)


def placed(distance, shift, table, index):
    total = jnp.zeros(distance.shape, F32)
    for k in range(8):
        total = jnp.where(distance == shift + k, table[index, k], total)
    return total


def lane_band_of(shift, table, index):
    lane = iota((8, 128), 1)
    base = placed(jnp.where(lane == 0, 0, 128 - lane), shift, table, index)
    turned = pltpu.roll(jnp.broadcast_to(base[:1], (128, 128)), 0, 1, stride=1, stride_axis=0)
    upper = iota((128, 128), 1) <= iota((128, 128), 0)
    return jnp.concatenate(
        [jnp.where(upper, turned, 0.0), jnp.where(upper, 0.0, turned)], axis=0
    ).astype(BF)


def filtered(image, row_band, lane_band):
    rows = row_band.shape[0]
    fit = dot(row_band, image).astype(BF)
    last = jnp.concatenate([fit[:, 256:], jnp.zeros((rows, 128), BF)], axis=1)
    found = dot(jnp.concatenate([fit[:, :256], fit[:, 128:], last], axis=0), lane_band)
    return jnp.concatenate([found[:rows], found[rows : 2 * rows], found[2 * rows :]], axis=1)


def crossed(value):
    turned = pltpu.roll(value, WIN, 1)
    return jnp.where(iota(value.shape, 1) < WIN, -turned, turned)


def look_matrix():
    lane = iota((LANES, 128), 0)
    col = jnp.where(lane < WIN, lane, lane - WIN)
    distance = col - LOOK_C * iota((LANES, 128), 1)
    inside = (col < SLAB) & (distance >= 0) & (distance < LOOK_C)
    return jnp.where(inside, 1.0, 0.0).astype(BF)


def looks_of(sums, looks):
    high = sums.astype(BF)
    low = (sums - high.astype(F32)).astype(BF)
    return dot(high, looks) + dot(low, looks)


def row_sum(first, second):
    rows = first.shape[0] // LOOK_R
    total = None
    for j in range(LOOK_R):
        part = first[j * rows : (j + 1) * rows].astype(F32) * second[j * rows : (j + 1) * rows].astype(F32)
        total = part if total is None else total + part
    return total


def pack_kernel(coarse, fraction, x, out, wide, packed, shifts, taps, in_sem, out_sem, small_sem):
    _, _, rows, cols = x.shape
    pieces = in_sem.shape[0] // 2
    width = cols // pieces
    small = [
        pltpu.make_async_copy(coarse, shifts, small_sem.at[0]),
        pltpu.make_async_copy(fraction, taps, small_sem.at[1]),
    ]
    incoming = [
        pltpu.make_async_copy(
            x.at[0, p, :, pl.ds(c * width, width)],
            wide.at[p, :, pl.ds(128 + c * width, width)],
            in_sem.at[2 * c + p],
        )
        for c in range(pieces)
        for p in range(2)
    ]
    for copy in small + incoming:
        copy.start()
    for p in range(2):
        wide[p, :, :128] = jnp.zeros((rows, 128), BF)
        wide[p, :, 128 + cols :] = jnp.zeros((rows, 128), BF)
    lane = iota((rows, LANES), 1)
    row = iota((rows, LANES), 0)
    for copy in small:
        copy.wait()
    own = jnp.where(row == 0, shifts[0, 0], jnp.where(row == 1, shifts[0, 1], 0))
    own = jnp.where(row == 2, taps[0, 0], jnp.where(row == 3, taps[0, 1], own))
    own = own.astype(F32)
    here = 0
    outgoing = []
    for j in range(out.shape[0]):
        start = 128 + SLAB * j - LEAD
        base, off = start // 128 * 128, start % 128
        while here < pieces and 128 + here * width < base + LANES:
            incoming[2 * here].wait()
            incoming[2 * here + 1].wait()
            here += 1
        first = pltpu.roll(wide[0, :, base : base + LANES].astype(F32), (LANES - off) % LANES, 1)
        second = pltpu.roll(wide[1, :, base : base + LANES].astype(F32), WIN - off, 1)
        value = jnp.where(lane < WIN, first, second)
        packed[j] = jnp.where(lane == SPARE, own, value).astype(BF)
        outgoing.append(pltpu.make_async_copy(packed.at[j], out.at[j], out_sem.at[j]))
        outgoing[-1].start()
    for copy in outgoing:
        copy.wait()


def candidate_kernel(image, out):
    rows = image.shape[0]
    order = jnp.where(row_order(rows, rows) == iota((rows, rows), 1), 1.0, 0.0).astype(BF)
    shift = jnp.where(iota((256, 128), 0) - iota((256, 128), 1) == LEAD, 1.0, 0.0).astype(BF)
    value = filtered(image[...], order, shift).astype(BF)
    for t in range(LANES // 128):
        out[t * rows : (t + 1) * rows] = value[:, t * 128 : (t + 1) * 128]


def resampled(image, offsets, n, table, rows_apart):
    row_band = placed(rows_apart, offsets[n, 0] - 3, table, offsets[n, 2]).astype(BF)
    lane_band = lane_band_of(LEAD + offsets[n, 1] - 3, table, offsets[n, 3])
    return filtered(image, row_band, lane_band)


def add_pairs(out, start, pairs, looks):
    sums = []
    for _, _, first, second, turned, _ in pairs:
        sums.append(row_sum(first, second))
        sums.append(row_sum(first, turned))
    count = sums[0].shape[0]
    maps = looks_of(jnp.concatenate(sums, axis=0), looks)
    totals = dict(start)
    for i, (n, s, _, _, _, power) in enumerate(pairs):
        for c in range(2):
            one = maps[(2 * i + c) * count : (2 * i + c + 1) * count]
            one = pltpu.roll(one, SLOT * (2 + 2 * s + c), 1)
            totals[n] = totals[n] + one if n in totals else one
        totals[n] = totals[n] + pltpu.roll(power, SLOT * (3 + 2 * SPAN + s), 1)
    for n, total in totals.items():
        out[n] = total


def resample_kernel(offsets, table, images, edges, z, turned, powers):
    dates, rows, _ = images.shape
    rows_apart = row_distance(rows)
    sums = []
    for n in range(dates):
        image = jnp.concatenate([images[n], edges[n]], axis=0)
        value = resampled(image, offsets, n, table, rows_apart)
        z[n] = value.astype(BF)
        turned[n] = crossed(value).astype(BF)
        sums.append(row_sum(z[n], z[n]))
    powers[...] = looks_of(jnp.concatenate(sums, axis=0), look_matrix()).reshape(powers.shape)


def own_kernel(z, turned, powers, out):
    dates = z.shape[0] // RUNS
    looks = look_matrix()
    for run in range(0, z.shape[0], dates):
        start = {n: pltpu.roll(powers[n], SLOT * (2 + 2 * SPAN), 1) for n in range(run, run + dates)}
        pairs = [
            (n, s, z[n], z[n + s + 1], turned[n + s + 1], powers[n + s + 1])
            for n in range(run, run + dates)
            for s in range(SPAN)
            if n + s + 1 < run + dates
        ]
        add_pairs(out, start, pairs, looks)


def later_kernel(offsets, table, later, edges, z, out):
    rows = z.shape[1]
    members = z.shape[0] // RUNS
    looks = look_matrix()
    rows_apart = row_distance(rows)
    last = lax.axis_index("z") == lax.axis_size("z") - 1
    found, sums = [], []
    for run in range(RUNS):
        base = jnp.where(last, SPAN * (RUNS - 1), SPAN * run)
        for n in range(SPAN):
            image = jnp.concatenate([later[base + n], edges[base + n]], axis=0)
            value = resampled(image, offsets, base + n, table, rows_apart)
            image = value.astype(BF)
            sums.append(row_sum(image, image))
            found.append((image, crossed(value).astype(BF)))
    powers = looks_of(jnp.concatenate(sums, axis=0), looks)
    count = sums[0].shape[0]
    pairs = []
    for run in range(RUNS):
        for n in range(SPAN):
            first = z[(run + 1) * members - SPAN + n]
            for m in range(n + 1):
                at = run * SPAN + m
                power = powers[at * count : (at + 1) * count]
                pairs.append((run * SPAN + n, m - n + SPAN - 1, first) + found[at] + (power,))
    add_pairs(out, {}, pairs, looks)


def reference_kernel(ref, part, later_part, z, near, below, above, out):
    dates = part.shape[0]
    rows = z.shape[1]
    size, members = lax.axis_size("z"), dates // RUNS
    apart = (lax.axis_index("z") - ref[0] // members) % size
    from_below = (apart >= 2) & (apart <= 4)
    from_above = (apart >= 5) & (apart <= 6)
    tiles = []
    for t in range(LANES // 128):
        at = slice(t * rows, (t + 1) * rows)
        value = jnp.where(from_below, below[at].astype(F32), near[at].astype(F32))
        tiles.append(jnp.where(from_above, above[at].astype(F32), value))
    value = jnp.concatenate(tiles, axis=1)
    turned = crossed(value).astype(BF)
    value = value.astype(BF)
    sums = []
    for n in range(dates):
        sums.append(row_sum(z[n], value))
        sums.append(row_sum(z[n], turned))
    maps = looks_of(jnp.concatenate(sums, axis=0), look_matrix())
    count = sums[0].shape[0]
    for n in range(dates):
        at = 2 * n * count
        total = part[n] + maps[at : at + count] + pltpu.roll(maps[at + count : at + 2 * count], SLOT, 1)
        if n % members >= members - SPAN:
            total = total + later_part[n // members * SPAN + n % members - members + SPAN]
        out[n] = total


def finish_kernel(on, got, ref_ifg, pair_ifg, coherence):
    slabs, count, _ = got.shape
    date, dates = lax.axis_index(DATE), lax.axis_size(DATE)
    slab = iota((count, 128), 1) // SLOT

    def gathered(m):
        total = jnp.zeros((count, 128), F32)
        for j in range(slabs):
            moved = pltpu.roll(got[j], SLOT * ((j - m) % slabs), 1)
            total = jnp.where(slab == j, moved, total)
        return total * (1.0 / (LOOK_R * LOOK_C))

    ref_ifg[0, 0] = gathered(0)
    ref_ifg[0, 1] = gathered(1)
    own = jnp.sqrt(gathered(2 + 2 * SPAN) + EPS)
    for s in range(SPAN):
        usable = (on[0, s] == 1) & (date + s + 1 < dates)
        re, im = gathered(2 + 2 * s), gathered(3 + 2 * s)
        other = jnp.sqrt(gathered(3 + 2 * SPAN + s) + EPS)
        coh = jnp.sqrt(re * re + im * im) / (own * other)
        pair_ifg[0, s, 0] = jnp.where(usable, re, 0.0)
        pair_ifg[0, s, 1] = jnp.where(usable, im, 0.0)
        coherence[0, s] = jnp.where(usable, coh, 0.0)


SMEM = pl.BlockSpec(memory_space=pltpu.SMEM)
VMEM = pl.BlockSpec(memory_space=pltpu.VMEM)


def call(kernel, scalars, arrays, outs, flops, scratch=()):
    moved = sum(a.size * a.dtype.itemsize for a in arrays)
    out_shape = [jax.ShapeDtypeStruct(s, d) for s, d in outs]
    single = len(out_shape) == 1
    return pl.pallas_call(
        kernel,
        out_shape=out_shape[0] if single else out_shape,
        in_specs=[SMEM] * len(scalars) + [VMEM] * len(arrays),
        out_specs=VMEM if single else [VMEM] * len(out_shape),
        scratch_shapes=list(scratch),
        compiler_params=pltpu.CompilerParams(vmem_limit_bytes=40 * 2**20),
        cost_estimate=pl.CostEstimate(flops=flops, bytes_accessed=moved, transcendentals=0),
    )(*scalars, *arrays)


def on_device(table, slc, coarse, fraction, pair_on, ref_date):
    _, _, rows, cols = slc.shape
    slabs = lax.axis_size(NEAR)
    members = slabs // RUNS
    size = lax.axis_size("z")
    count = rows // LOOK_R
    row = lax.axis_index("row")
    ref = ref_date[0]

    anywhere = pl.BlockSpec(memory_space=pl.ANY)
    packed = pl.pallas_call(
        pack_kernel,
        out_shape=jax.ShapeDtypeStruct((slabs, rows, LANES), BF),
        in_specs=[anywhere] * 3,
        out_specs=anywhere,
        scratch_shapes=[
            pltpu.VMEM((2, rows, cols + 256), BF),
            pltpu.VMEM((slabs, rows, LANES), BF),
            pltpu.SMEM((1, 2), jnp.int32),
            pltpu.SMEM((1, 2), jnp.int32),
            pltpu.SemaphoreType.DMA((8,)),
            pltpu.SemaphoreType.DMA((slabs,)),
            pltpu.SemaphoreType.DMA((2,)),
        ],
        compiler_params=pltpu.CompilerParams(vmem_limit_bytes=60 * 2**20),
        cost_estimate=pl.CostEstimate(flops=10**8, bytes_accessed=2 * 10**6, transcendentals=0),
    )(coarse, fraction, slc)
    images = lax.all_to_all(packed, NEAR, 0, 0)

    edge = jnp.where(row == 0, images[:, rows - HALO :], images[:, :HALO])
    edges = lax.ppermute(edge, "row", [(0, 1), (1, 0)])

    def first_dates(value):
        return jnp.concatenate([value[n : n + SPAN] for n in range(0, slabs, members)], axis=0)

    later = lax.ppermute(first_dates(images), "z", [((i + 1) % size, i) for i in range(size)])
    later_edges = lax.ppermute(
        first_dates(edge), ("z", "row"),
        [((i + 1) % size * 2 + 1 - r, i * 2 + r) for i in range(size) for r in range(2)],
    )

    cand = lax.dynamic_index_in_dim(
        images, ref // (members * size) * members + ref % members, 0, keepdims=False
    )
    q = call(candidate_kernel, [], [cand], [((LANES // 128 * rows, 128), BF)], 10**10)

    def around(value, by):
        return lax.ppermute(value, "z", [(i, (i + by) % size) for i in range(size)])

    apart = (lax.axis_index("z") - ref // members) % size
    below, above = around(q, 1), around(q, -1)

    sums = (slabs, count, 128)
    offsets = images[:, :4, SPARE].astype(jnp.int32)
    z, turned, powers = call(
        resample_kernel, [offsets, table], [images, edges],
        [(images.shape, BF), (images.shape, BF), (sums, F32)], 4 * 10**9,
    )
    below, z = lax.optimization_barrier((below, z))
    near = jnp.where(apart == 1, below, jnp.where(apart == size - 1, above, q))
    below, above = around(near, 3), around(near, -3)
    part = call(own_kernel, [], [z, turned, powers], [(sums, F32)], 2 * 10**9)
    later_offsets = later[:, :4, SPARE].astype(jnp.int32)
    later_part = call(
        later_kernel, [later_offsets, table], [later, later_edges, z],
        [((RUNS * SPAN, count, 128), F32)], 2 * 10**9,
    )
    maps = call(
        reference_kernel, [ref_date], [part, later_part, z, near, below, above],
        [(sums, F32)], 10**9,
    )
    got = lax.all_to_all(maps, NEAR, 0, 0)
    small = (count, 128)
    return call(
        finish_kernel, [pair_on], [got],
        [((1, 2) + small, F32), ((1, SPAN, 2) + small, F32), ((1, SPAN) + small, F32)], 10**7,
    )


def solution(mesh):
    shape = GRID + (mesh.shape["row"],)
    grid = Mesh(mesh.devices.reshape(shape), DATE + ("row",))
    table = tap_table()

    def program(slc, coarse, fraction, pair_on, ref_date):
        return tuple(
            jax.shard_map(
                on_device,
                mesh=grid,
                in_specs=(
                    P(),
                    P(DATE, None, "row", None),
                    P(DATE, None),
                    P(DATE, None),
                    P(DATE, None),
                    P(),
                ),
                out_specs=(
                    P(DATE, None, "row", None),
                    P(DATE, None, None, "row", None),
                    P(DATE, None, "row", None),
                ),
                check_vma=False,
            )(jnp.asarray(table), slc, coarse, fraction, pair_on, ref_date)
        )

    return program
```

```python
import jax
import jax.numpy as jnp
import ml_dtypes
import numpy as np
from jax import lax
from jax.experimental import pallas as pl
from jax.experimental.pallas import tpu as pltpu
from jax.sharding import Mesh, PartitionSpec as P

NFRAC = 64
SPAN = 3
LOOK_R = 5
LOOK_C = 20
EPS = 1e-06
BF = jnp.bfloat16
F32 = jnp.float32

GRID = (2, 8, 4, 2)
DATE = ("xl", "z", "y", "core")
NEAR = ("xl", "y", "core")
RUNS = 2
HALO = 16

SLAB = 160
WIN = 192
LEAD = 16
LANES = 2 * WIN
SPARE = 190
SLOT = SLAB // LOOK_C


def tap_table():
    x = np.arange(8)[None, :] - 3.0 - np.arange(NFRAC)[:, None] / NFRAC
    w = np.sinc(x) * (0.54 + 0.46 * np.cos(np.pi * x / 4.0))
    taps = (w / w.sum(axis=1, keepdims=True)).astype(np.float32)
    return taps.astype(ml_dtypes.bfloat16).astype(np.float32)


def iota(shape, dim):
    return lax.broadcasted_iota(jnp.int32, shape, dim)


def dot(a, b):
    return jnp.dot(a, b, preferred_element_type=F32)


def row_order(rows, columns):
    looks = rows // LOOK_R
    out = iota((rows, columns), 0)
    return (out % looks) * LOOK_R + out // looks


def row_distance(rows):
    source = iota((rows, rows + HALO), 1)
    first = lax.axis_index("row") == 0
    source = jnp.where((source < rows) | first, source, source - rows - HALO)
    return source - row_order(rows, rows + HALO)


def placed(distance, shift, table, index):
    total = jnp.zeros(distance.shape, F32)
    for k in range(8):
        total = jnp.where(distance == shift + k, table[8 * index + k], total)
    return total


def lane_band_of(shift, table, index):
    lane = iota((8, 128), 1)
    base = placed(jnp.where(lane == 0, 0, 128 - lane), shift, table, index)
    turned = pltpu.roll(jnp.broadcast_to(base[:1], (128, 128)), 0, 1, stride=1, stride_axis=0)
    upper = iota((128, 128), 1) <= iota((128, 128), 0)
    return jnp.concatenate(
        [jnp.where(upper, turned, 0.0), jnp.where(upper, 0.0, turned)], axis=0
    ).astype(BF)


def filtered(image, row_band, lane_band):
    rows = row_band.shape[0]
    fit = dot(row_band, image).astype(BF)
    last = jnp.concatenate([fit[:, 256:], jnp.zeros((rows, 128), BF)], axis=1)
    found = dot(jnp.concatenate([fit[:, :256], fit[:, 128:], last], axis=0), lane_band)
    return jnp.concatenate([found[:rows], found[rows : 2 * rows], found[2 * rows :]], axis=1)


def crossed(value):
    turned = pltpu.roll(value, WIN, 1)
    return jnp.where(iota(value.shape, 1) < WIN, -turned, turned)


def look_matrix():
    lane = iota((LANES, 128), 0)
    col = jnp.where(lane < WIN, lane, lane - WIN)
    distance = col - LOOK_C * iota((LANES, 128), 1)
    inside = (col < SLAB) & (distance >= 0) & (distance < LOOK_C)
    return jnp.where(inside, 1.0, 0.0).astype(BF)


def looks_of(sums, looks):
    high = sums.astype(BF)
    low = (sums - high.astype(F32)).astype(BF)
    return dot(high, looks) + dot(low, looks)


def row_sum(first, second):
    rows = first.shape[0] // LOOK_R
    total = None
    for j in range(LOOK_R):
        part = first[j * rows : (j + 1) * rows].astype(F32) * second[j * rows : (j + 1) * rows].astype(F32)
        total = part if total is None else total + part
    return total


def pack_kernel(coarse, fraction, x, out, wide, packed, shifts, taps, in_sem, out_sem, small_sem):
    _, _, rows, cols = x.shape
    pieces = in_sem.shape[0] // 2
    width = cols // pieces
    small = [
        pltpu.make_async_copy(coarse, shifts, small_sem.at[0]),
        pltpu.make_async_copy(fraction, taps, small_sem.at[1]),
    ]
    incoming = [
        pltpu.make_async_copy(
            x.at[0, p, :, pl.ds(c * width, width)],
            wide.at[p, :, pl.ds(128 + c * width, width)],
            in_sem.at[2 * c + p],
        )
        for c in range(pieces)
        for p in range(2)
    ]
    for copy in small + incoming:
        copy.start()
    for p in range(2):
        wide[p, :, :128] = jnp.zeros((rows, 128), BF)
        wide[p, :, 128 + cols :] = jnp.zeros((rows, 128), BF)
    lane = iota((rows, LANES), 1)
    row = iota((rows, LANES), 0)
    for copy in small:
        copy.wait()
    own = jnp.where(row == 0, shifts[0, 0], jnp.where(row == 1, shifts[0, 1], 0))
    own = jnp.where(row == 2, taps[0, 0], jnp.where(row == 3, taps[0, 1], own))
    own = own.astype(F32).astype(BF)
    here = 0
    outgoing = []
    for j in range(out.shape[0]):
        start = 128 + SLAB * j - LEAD
        base, off = start // 128 * 128, start % 128
        while here < pieces and 128 + here * width < base + LANES:
            incoming[2 * here].wait()
            incoming[2 * here + 1].wait()
            here += 1
        first = pltpu.roll(wide[0, :, base : base + LANES], (LANES - off) % LANES, 1)
        second = pltpu.roll(wide[1, :, base : base + LANES], WIN - off, 1)
        value = jnp.where(lane < WIN, first, second)
        packed[j] = jnp.where(lane == SPARE, own, value)
        outgoing.append(pltpu.make_async_copy(packed.at[j], out.at[j], out_sem.at[j]))
        outgoing[-1].start()
    for copy in outgoing:
        copy.wait()


def candidate_kernel(image, out):
    rows = image.shape[0]
    order = jnp.where(row_order(rows, rows) == iota((rows, rows), 1), 1.0, 0.0).astype(BF)
    shift = jnp.where(iota((256, 128), 0) - iota((256, 128), 1) == LEAD, 1.0, 0.0).astype(BF)
    value = filtered(image[...], order, shift).astype(BF)
    for t in range(LANES // 128):
        out[t * rows : (t + 1) * rows] = value[:, t * 128 : (t + 1) * 128]


def resampled(image, offsets, n, table, rows_apart):
    row_band = placed(rows_apart, offsets[n, 0] - 3, table, offsets[n, 2]).astype(BF)
    lane_band = lane_band_of(LEAD + offsets[n, 1] - 3, table, offsets[n, 3])
    return filtered(image, row_band, lane_band)


def add_pairs(out, start, pairs, looks):
    sums = []
    for _, _, first, second, turned, _ in pairs:
        sums.append(row_sum(first, second))
        sums.append(row_sum(first, turned))
    count = sums[0].shape[0]
    maps = looks_of(jnp.concatenate(sums, axis=0), looks)
    totals = dict(start)
    for i, (n, s, _, _, _, power) in enumerate(pairs):
        for c in range(2):
            one = maps[(2 * i + c) * count : (2 * i + c + 1) * count]
            one = pltpu.roll(one, SLOT * (2 + 2 * s + c), 1)
            totals[n] = totals[n] + one if n in totals else one
        totals[n] = totals[n] + pltpu.roll(power, SLOT * (3 + 2 * SPAN + s), 1)
    for n, total in totals.items():
        out[n] = total


def resample_kernel(offsets, table, images, edges, z, turned, powers):
    dates, rows, _ = images.shape
    rows_apart = row_distance(rows)
    sums = []
    for n in range(dates):
        image = jnp.concatenate([images[n], edges[n]], axis=0)
        value = resampled(image, offsets, n, table, rows_apart)
        z[n] = value.astype(BF)
        turned[n] = crossed(value).astype(BF)
        sums.append(row_sum(z[n], z[n]))
    powers[...] = looks_of(jnp.concatenate(sums, axis=0), look_matrix()).reshape(powers.shape)


def own_kernel(z, turned, powers, out):
    dates = z.shape[0] // RUNS
    looks = look_matrix()
    for run in range(0, z.shape[0], dates):
        start = {n: pltpu.roll(powers[n], SLOT * (2 + 2 * SPAN), 1) for n in range(run, run + dates)}
        pairs = [
            (n, s, z[n], z[n + s + 1], turned[n + s + 1], powers[n + s + 1])
            for n in range(run, run + dates)
            for s in range(SPAN)
            if n + s + 1 < run + dates
        ]
        add_pairs(out, start, pairs, looks)


def later_kernel(offsets, table, later, edges, z, out):
    rows = z.shape[1]
    members = z.shape[0] // RUNS
    looks = look_matrix()
    rows_apart = row_distance(rows)
    last = lax.axis_index("z") == lax.axis_size("z") - 1
    found, sums = [], []
    for run in range(RUNS):
        base = jnp.where(last, SPAN * (RUNS - 1), SPAN * run)
        for n in range(SPAN):
            image = jnp.concatenate([later[base + n], edges[base + n]], axis=0)
            value = resampled(image, offsets, base + n, table, rows_apart)
            image = value.astype(BF)
            sums.append(row_sum(image, image))
            found.append((image, crossed(value).astype(BF)))
    powers = looks_of(jnp.concatenate(sums, axis=0), looks)
    count = sums[0].shape[0]
    pairs = []
    for run in range(RUNS):
        for n in range(SPAN):
            first = z[(run + 1) * members - SPAN + n]
            for m in range(n + 1):
                at = run * SPAN + m
                power = powers[at * count : (at + 1) * count]
                pairs.append((run * SPAN + n, m - n + SPAN - 1, first) + found[at] + (power,))
    add_pairs(out, {}, pairs, looks)


def reference_kernel(ref, part, later_part, z, near, below, above, out):
    dates = part.shape[0]
    rows = z.shape[1]
    size, members = lax.axis_size("z"), dates // RUNS
    apart = (lax.axis_index("z") - ref[0] // members) % size
    from_below = (apart >= 2) & (apart <= 4)
    from_above = (apart >= 5) & (apart <= 6)
    tiles = []
    for t in range(LANES // 128):
        at = slice(t * rows, (t + 1) * rows)
        value = jnp.where(from_below, below[at].astype(F32), near[at].astype(F32))
        tiles.append(jnp.where(from_above, above[at].astype(F32), value))
    value = jnp.concatenate(tiles, axis=1)
    turned = crossed(value).astype(BF)
    value = value.astype(BF)
    sums = []
    for n in range(dates):
        sums.append(row_sum(z[n], value))
        sums.append(row_sum(z[n], turned))
    maps = looks_of(jnp.concatenate(sums, axis=0), look_matrix())
    count = sums[0].shape[0]
    for n in range(dates):
        at = 2 * n * count
        total = part[n] + maps[at : at + count] + pltpu.roll(maps[at + count : at + 2 * count], SLOT, 1)
        if n % members >= members - SPAN:
            total = total + later_part[n // members * SPAN + n % members - members + SPAN]
        out[n] = total


def finish_kernel(on, got, ref_ifg, pair_ifg, coherence):
    slabs, count, lanes = got.shape
    date, dates = lax.axis_index(DATE), lax.axis_size(DATE)
    slab = iota((count, lanes), 1) // SLOT
    maps = [got[j] for j in range(slabs)]
    step = 1
    while step < slabs:
        low = slab // step % 2 == 0
        moved = []
        for j in range(slabs):
            if j // step % 2 == 0:
                moved.append(jnp.where(low, maps[j], pltpu.roll(maps[j + step], SLOT * step, 1)))
            else:
                moved.append(jnp.where(low, pltpu.roll(maps[j - step], lanes - SLOT * step, 1), maps[j]))
        maps = moved
        step *= 2

    def gathered(m):
        return maps[m] * (1.0 / (LOOK_R * LOOK_C))

    ref_ifg[0, 0] = gathered(0)
    ref_ifg[0, 1] = gathered(1)
    own = jnp.sqrt(gathered(2 + 2 * SPAN) + EPS)
    for s in range(SPAN):
        usable = (on[0, s] == 1) & (date + s + 1 < dates)
        re, im = gathered(2 + 2 * s), gathered(3 + 2 * s)
        other = jnp.sqrt(gathered(3 + 2 * SPAN + s) + EPS)
        coh = jnp.sqrt(re * re + im * im) / (own * other)
        pair_ifg[0, s, 0] = jnp.where(usable, re, 0.0)
        pair_ifg[0, s, 1] = jnp.where(usable, im, 0.0)
        coherence[0, s] = jnp.where(usable, coh, 0.0)


SMEM = pl.BlockSpec(memory_space=pltpu.SMEM)
VMEM = pl.BlockSpec(memory_space=pltpu.VMEM)


def call(kernel, scalars, arrays, outs, flops, scratch=()):
    moved = sum(a.size * a.dtype.itemsize for a in arrays)
    out_shape = [jax.ShapeDtypeStruct(s, d) for s, d in outs]
    single = len(out_shape) == 1
    return pl.pallas_call(
        kernel,
        out_shape=out_shape[0] if single else out_shape,
        in_specs=[SMEM] * len(scalars) + [VMEM] * len(arrays),
        out_specs=VMEM if single else [VMEM] * len(out_shape),
        scratch_shapes=list(scratch),
        compiler_params=pltpu.CompilerParams(vmem_limit_bytes=40 * 2**20),
        cost_estimate=pl.CostEstimate(flops=flops, bytes_accessed=moved, transcendentals=0),
    )(*scalars, *arrays)


def on_device(table, slc, coarse, fraction, pair_on, ref_date):
    _, _, rows, cols = slc.shape
    slabs = lax.axis_size(NEAR)
    members = slabs // RUNS
    size = lax.axis_size("z")
    count = rows // LOOK_R
    row = lax.axis_index("row")
    ref = ref_date[0]

    anywhere = pl.BlockSpec(memory_space=pl.ANY)
    packed = pl.pallas_call(
        pack_kernel,
        out_shape=jax.ShapeDtypeStruct((slabs, rows, LANES), BF),
        in_specs=[anywhere] * 3,
        out_specs=anywhere,
        scratch_shapes=[
            pltpu.VMEM((2, rows, cols + 256), BF),
            pltpu.VMEM((slabs, rows, LANES), BF),
            pltpu.SMEM((1, 2), jnp.int32),
            pltpu.SMEM((1, 2), jnp.int32),
            pltpu.SemaphoreType.DMA((8,)),
            pltpu.SemaphoreType.DMA((slabs,)),
            pltpu.SemaphoreType.DMA((2,)),
        ],
        compiler_params=pltpu.CompilerParams(vmem_limit_bytes=60 * 2**20),
        cost_estimate=pl.CostEstimate(flops=10**8, bytes_accessed=2 * 10**6, transcendentals=0),
    )(coarse, fraction, slc)
    images = lax.all_to_all(packed, NEAR, 0, 0)

    edge = jnp.where(row == 0, images[:, rows - HALO :], images[:, :HALO])
    edges = lax.ppermute(edge, "row", [(0, 1), (1, 0)])

    def first_dates(value):
        return jnp.concatenate([value[n : n + SPAN] for n in range(0, slabs, members)], axis=0)

    later = lax.ppermute(first_dates(images), "z", [((i + 1) % size, i) for i in range(size)])
    later_edges = lax.ppermute(
        first_dates(edge), ("z", "row"),
        [((i + 1) % size * 2 + 1 - r, i * 2 + r) for i in range(size) for r in range(2)],
    )

    cand = lax.dynamic_index_in_dim(
        images, ref // (members * size) * members + ref % members, 0, keepdims=False
    )
    q = call(candidate_kernel, [], [cand], [((LANES // 128 * rows, 128), BF)], 10**10)

    def around(value, by):
        return lax.ppermute(value, "z", [(i, (i + by) % size) for i in range(size)])

    apart = (lax.axis_index("z") - ref // members) % size
    below, above = around(q, 1), around(q, -1)

    sums = (slabs, count, 128)
    offsets = images[:, :4, SPARE].astype(jnp.int32)
    z, turned, powers = call(
        resample_kernel, [offsets, table], [images, edges],
        [(images.shape, BF), (images.shape, BF), (sums, F32)], 4 * 10**9,
    )
    below, z = lax.optimization_barrier((below, z))
    near = jnp.where(apart == 1, below, jnp.where(apart == size - 1, above, q))
    below, above = around(near, 3), around(near, -3)
    part = call(own_kernel, [], [z, turned, powers], [(sums, F32)], 2 * 10**9)
    later_offsets = later[:, :4, SPARE].astype(jnp.int32)
    later_part = call(
        later_kernel, [later_offsets, table], [later, later_edges, z],
        [((RUNS * SPAN, count, 128), F32)], 2 * 10**9,
    )
    maps = call(
        reference_kernel, [ref_date], [part, later_part, z, near, below, above],
        [(sums, F32)], 10**9,
    )
    got = lax.all_to_all(maps, NEAR, 0, 0)
    small = (count, 128)
    return call(
        finish_kernel, [pair_on], [got],
        [((1, 2) + small, F32), ((1, SPAN, 2) + small, F32), ((1, SPAN) + small, F32)], 10**7,
    )


def solution(mesh):
    shape = GRID + (mesh.shape["row"],)
    grid = Mesh(mesh.devices.reshape(shape), DATE + ("row",))
    table = tap_table()

    def program(slc, coarse, fraction, pair_on, ref_date):
        return tuple(
            jax.shard_map(
                on_device,
                mesh=grid,
                in_specs=(
                    P(),
                    P(DATE, None, "row", None),
                    P(DATE, None),
                    P(DATE, None),
                    P(DATE, None),
                    P(),
                ),
                out_specs=(
                    P(DATE, None, "row", None),
                    P(DATE, None, None, "row", None),
                    P(DATE, None, "row", None),
                ),
                check_vma=False,
            )(jnp.asarray(table.reshape(-1)), slc, coarse, fraction, pair_on, ref_date)
        )

    return program
```
